32 devices in a mesh: groups: 2 (over y), expert: 8 (over z, x), dp: 2 (over core).
Axes of the slice: x: 2, y: 2, z: 4, core: 2. Of those that a mesh axis runs over, the one named last changes fastest.
Arguments:
- tokens: bfloat16 [4096, 2048], P(('groups', 'expert', 'dp')), parts along dimension 0, may hold values from -6 to 6
- cotangent: bfloat16 [4096, 2048], P(('groups', 'expert', 'dp')), parts along dimension 0, may hold values from -6 to 6
- routes: int32 [4096, 4], P(('groups', 'expert', 'dp')), parts along dimension 0, may hold values from 0 to 15, as said below
- gates: float32 [4096, 4], P(('groups', 'expert', 'dp')), parts along dimension 0, may hold values from 0.05 to 0.6
- helper: int32 [32], P('groups'), parts along dimension 0, may hold values from 0 to 1
- w_gate: bfloat16 [16, 2048, 384], P(('expert', 'dp')), may hold values from -0.125 to 0.125
- w_up: bfloat16 [16, 2048, 384], P(('expert', 'dp')), may hold values from -0.125 to 0.125
- w_down: bfloat16 [16, 384, 2048], P(('expert', 'dp')), may hold values from -0.3125 to 0.3125
Outputs:
- grad_tokens: bfloat16 [4096, 2048], P(('groups', 'expert', 'dp')), parts along dimension 0
- grad_gate: bfloat16 [32, 2048, 384], P(('groups', 'expert', 'dp')), parts along dimension 0
- grad_up: bfloat16 [32, 2048, 384], P(('groups', 'expert', 'dp')), parts along dimension 0
- grad_down: bfloat16 [32, 384, 2048], P(('groups', 'expert', 'dp')), parts along dimension 0
The draws below stay inside these ranges and needn't reach their ends.
There are 2 independent parts, one for each index of `groups`. The reference program is written for one: setup_inputs(seed, part) draws one part's arguments, and reference() takes and returns one part's arrays. A program takes and returns all parts, laid end to end along the dimension named above; an argument that names none is the same for every part. Nothing has to cross between parts.
Inputs may be any that keep to these rules, and one draw needn't show every extreme that they name: `routes`: each row names 4 different experts; the rows of one device name no expert more than 64 times, and some expert exactly 64 times in the rows of every device.
All inputs are finite; a program needn't handle non-finite values.
Results may differ from the reference program's by a relative error of at most 0.0065.
Values may be sent and summed in bfloat16 or wider, within the bound.
No kernel may reach another device: no remote copies, remote signals or barrier semaphores. Data moves between devices by JAX's collectives and lax.ppermute only.
A program may use at most 128 MiB of HBM per device.

```python
import math
import jax
import jax.numpy as jnp
from jax import lax

D = 2048
HIDDEN_SIZE = 384
TOP_K = 4
TOK_DEV = 128
EXPERTS = 16
TOKENS = 2048
ROUTE_CAP = 64
HOME_CAP = 40


def expert_order(key):
    return jax.random.permutation(jax.random.fold_in(key, 7), EXPERTS).astype(jnp.int32)


def draw_routes(key, part):
    order = expert_order(key)
    busiest = max(1, EXPERTS // 16)
    block_rows = TOK_DEV * TOP_K
    spare = block_rows - busiest * ROUTE_CAP
    others = EXPERTS - busiest
    spread = max(0, (spare // others - 1) // 2)

    def one_block(block):
        block_key = jax.random.fold_in(jax.random.fold_in(key, 13), block)
        key_edge, key_cold, key_group, key_token = jax.random.split(block_key, 4)
        edges = jnp.arange(others + 1, dtype=jnp.int32) * spare // others
        jitter = jax.random.randint(key_edge, (others + 1,), -spread, spread + 1).astype(jnp.int32)
        jitter = jitter.at[0].set(0).at[others].set(0)
        edges = edges + jitter
        cold_sizes = edges[1:] - edges[:-1]
        cold_perm = jax.random.permutation(key_cold, others)
        counts = jnp.zeros((EXPERTS,), jnp.int32).at[order[:busiest]].set(ROUTE_CAP)
        counts = counts.at[order[busiest:][cold_perm]].set(cold_sizes)
        group = jax.random.permutation(key_group, EXPERTS).astype(jnp.int32)
        bounds = jnp.cumsum(counts[group])
        place = jnp.arange(block_rows, dtype=jnp.int32)
        which = jnp.searchsorted(bounds, place, side='right')
        layout = group[which]
        grid = layout.reshape(TOP_K, TOK_DEV).T
        token_perm = jax.random.permutation(key_token, TOK_DEV)
        return jnp.zeros_like(grid).at[token_perm].set(grid)
    blocks = jax.vmap(one_block)(jnp.arange(EXPERTS, dtype=jnp.int32))
    return blocks.reshape(TOKENS, TOP_K).astype(jnp.int32)


def draw_helper(key, part):
    order = expert_order(key)
    flags = jax.random.randint(jax.random.fold_in(key, 17), (EXPERTS,), 0, 2).astype(jnp.int32)
    flags = flags.at[jnp.bitwise_xor(order[0], 1)].set(1)
    if max(1, EXPERTS // 16) > 1:
        flags = flags.at[jnp.bitwise_xor(order[1], 1)].set(0)
    return flags.astype(jnp.int32)


def level_of(own_key, extent, cuts, smallest, largest):
    level, own = 1.0, jax.random.fold_in(own_key, 6)
    for axis_at, shards_of in cuts:
        draws = jnp.exp(jax.random.uniform(jax.random.fold_in(own, axis_at), (shards_of,), jnp.float32, smallest / len(cuts), largest / len(cuts)))
        level = level * jnp.repeat(draws, extent[axis_at] // shards_of).reshape([-1 if axis == axis_at else 1 for axis in range(len(extent))])
    return level


def scatter_about(own_key, dims, scale, limit, pieces=(), kind=jnp.bfloat16):
    level = level_of(own_key, dims, pieces, -0.22, 0.18) if pieces else 1.0
    drawn = jax.random.normal(own_key, dims, jnp.float32) * scale * level
    return jnp.minimum(jnp.maximum(drawn, -limit), limit).astype(kind)


def setup_inputs(seed: int = 0, part: int = 0) -> dict:
    arg_keys = jax.random.split(jax.random.key(seed), 9)
    own_keys = jax.random.split(jax.random.fold_in(arg_keys[8], part), 9)
    tokens = scatter_about(own_keys[0], (TOKENS, D), 1.0, 6.0, ((0, 16),))
    cotangent = scatter_about(own_keys[1], (TOKENS, D), 0.5, 6.0, ((0, 16),))
    routes = draw_routes(jax.random.fold_in(jax.random.fold_in(arg_keys[8], part), 71), part)
    gates = jnp.clip(jnp.exp(math.log(0.6) - 2.4849067 * jax.random.uniform(own_keys[3], (TOKENS, TOP_K), jnp.float32) ** level_of(own_keys[3], (TOKENS, TOP_K), ((0, 16),), -0.2, 0.2)), 0.05, 0.6)
    helper = draw_helper(jax.random.fold_in(jax.random.fold_in(arg_keys[8], part), 71), part)
    w_gate = scatter_about(arg_keys[5], (EXPERTS, D, HIDDEN_SIZE), D ** -0.5, 0.125, ((0, 16),))
    w_up = scatter_about(arg_keys[6], (EXPERTS, D, HIDDEN_SIZE), D ** -0.5, 0.125, ((0, 16),))
    w_down = scatter_about(arg_keys[7], (EXPERTS, HIDDEN_SIZE, D), HIDDEN_SIZE ** -0.5, 0.3125, ((0, 16),))
    return dict(tokens=tokens, cotangent=cotangent, routes=routes, gates=gates, helper=helper, w_gate=w_gate, w_up=w_up, w_down=w_down)


def expert_pass(rows, scaled, gate_w, up_w, down_w):
    gate_pre = jnp.dot(rows, gate_w, preferred_element_type=jnp.float32)
    up_pre = jnp.dot(rows, up_w, preferred_element_type=jnp.float32)
    sigma = jax.nn.sigmoid(gate_pre)
    active = gate_pre * sigma
    hidden = (active * up_pre).astype(jnp.bfloat16)
    over_last = (((1,), (1,)), ((), ()))
    over_rows = (((0,), (0,)), ((), ()))
    back_hidden = lax.dot_general(scaled, down_w, over_last, preferred_element_type=jnp.float32)
    grad_gating = (back_hidden * up_pre * sigma * (1.0 + gate_pre * (1.0 - sigma))).astype(jnp.bfloat16)
    grad_upward = (back_hidden * active).astype(jnp.bfloat16)
    grad_down = lax.dot_general(hidden, scaled, over_rows, preferred_element_type=jnp.float32)
    grad_gate = lax.dot_general(rows, grad_gating, over_rows, preferred_element_type=jnp.float32)
    grad_up = lax.dot_general(rows, grad_upward, over_rows, preferred_element_type=jnp.float32)
    row_grads = lax.dot_general(grad_gating, gate_w, over_last, preferred_element_type=jnp.float32)
    row_grads = row_grads + lax.dot_general(grad_upward, up_w, over_last, preferred_element_type=jnp.float32)
    return row_grads.astype(jnp.bfloat16), grad_gate, grad_up, grad_down


def reference(tokens, cotangent, routes, gates, helper, w_gate, w_up, w_down):
    block_rows = TOK_DEV * TOP_K
    routes_all = TOKENS * TOP_K
    experts_row = jnp.arange(EXPERTS, dtype=jnp.int32)

    def block_rank(block_ids):
        one_hot = (block_ids[:, None] == experts_row[None, :]).astype(jnp.float32)
        before = jnp.cumsum(one_hot, axis=0) - one_hot
        return jnp.sum(before * one_hot, axis=1).astype(jnp.int32)

    route_rank = lax.map(block_rank, routes.reshape(EXPERTS, block_rows)).reshape(routes_all)
    flat_ids = routes.reshape(routes_all)
    partner_flag = helper[jnp.bitwise_xor(flat_ids, 1)]
    kept = (route_rank < HOME_CAP) | (partner_flag == 1)
    route_index = jnp.arange(routes_all, dtype=jnp.int32)
    column = (route_index // block_rows) * ROUTE_CAP + route_rank
    row_target = jnp.where(kept, flat_ids, EXPERTS).astype(jnp.int32)
    table = jnp.full((EXPERTS, EXPERTS * ROUTE_CAP), routes_all, jnp.int32)
    table = table.at[row_target, column].set(route_index, mode="drop")
    tokens_pad = jnp.concatenate([tokens, jnp.zeros((1, D), jnp.bfloat16)], axis=0)
    cot_pad = jnp.concatenate([cotangent, jnp.zeros((1, D), jnp.bfloat16)], axis=0)
    gate_pad = jnp.concatenate([gates.reshape(routes_all), jnp.zeros((1,), jnp.float32)], axis=0)

    def per_expert(carry, inputs):
        source, gate_w, up_w, down_w = inputs
        token_of = jnp.where(source < routes_all, source // TOP_K, TOKENS).astype(jnp.int32)
        rows = tokens_pad[token_of]
        scaled = (cot_pad[token_of].astype(jnp.float32) * gate_pad[source][:, None]).astype(jnp.bfloat16)
        row_grads, grad_gate, grad_up, grad_down = expert_pass(rows, scaled, gate_w, up_w, down_w)
        carry = carry.at[token_of].add(row_grads.astype(jnp.float32))
        return carry, (grad_gate.astype(jnp.bfloat16), grad_up.astype(jnp.bfloat16), grad_down.astype(jnp.bfloat16))

    start = jnp.zeros((TOKENS + 1, D), jnp.float32)
    final, stacked = lax.scan(per_expert, start, (table, w_gate, w_up, w_down))
    return final[:TOKENS].astype(jnp.bfloat16), stacked[0], stacked[1], stacked[2]
```

```python
import functools

import jax
import jax.numpy as jnp
from jax import lax
from jax.experimental import pallas as pl
from jax.experimental.pallas import tpu as pltpu
from jax.sharding import PartitionSpec as P

OVER_LAST = (((1,), (1,)), ((), ()))
OVER_ROWS = (((0,), (0,)), ((), ()))
VMEM_LIMIT = 56 * 1024 * 1024


def ring_of(mesh):
    chips = list(mesh.devices[0, :, 0])
    places = [getattr(chip, "coords", None) for chip in chips]
    natural = list(range(len(chips)))
    if any(place is None for place in places):
        return natural
    at = {(place[0], place[2]): i for i, place in enumerate(places)}
    xs = sorted({x for x, _ in at})
    zs = sorted({z for _, z in at})
    if len(at) != len(chips) or len(xs) * len(zs) != len(chips):
        return natural
    if len(xs) == 2:
        return [at[xs[0], z] for z in zs] + [at[xs[1], z] for z in reversed(zs)]
    if len(zs) == 2:
        return [at[x, zs[0]] for x in xs] + [at[x, zs[1]] for x in reversed(xs)]
    return natural


def pack_kernel(home_cap, lanes, routes_ref, gates_ref, helper_ref, tokens_ref, out_ref):
    rows, width = tokens_ref.shape
    experts = helper_ref.shape[1]
    expert_of_row = lax.broadcasted_iota(jnp.int32, (experts, rows), 0)
    named = jnp.zeros((experts, rows), jnp.float32)
    gate = jnp.zeros((experts, rows), jnp.float32)
    for k in range(routes_ref.shape[0]):
        hit = routes_ref[k : k + 1, :] == expert_of_row
        named = named + jnp.where(hit, 1.0, 0.0)
        gate = gate + jnp.where(hit, gates_ref[k : k + 1, :], 0.0)
    earlier = lax.broadcasted_iota(jnp.int32, (rows, rows), 0) < lax.broadcasted_iota(
        jnp.int32, (rows, rows), 1
    )
    rank = jnp.dot(
        named.astype(jnp.bfloat16),
        jnp.where(earlier, 1.0, 0.0).astype(jnp.bfloat16),
        preferred_element_type=jnp.float32,
    )
    partner = jnp.bitwise_xor(lax.broadcasted_iota(jnp.int32, (experts, experts), 0), 1)
    column = lax.broadcasted_iota(jnp.int32, (experts, experts), 1)
    flag = jnp.where(partner == column, helper_ref[...], 0)
    helped = jnp.max(flag, axis=1, keepdims=True) == 1
    gate = jnp.where((rank < home_cap) | helped, gate, 0.0)
    terms = []
    for _ in range(3):
        term = gate.astype(jnp.bfloat16).astype(jnp.float32)
        terms.append(term)
        gate = gate - term
    terms.append(jnp.zeros((lanes - 3 * experts, rows), jnp.float32))
    out_ref[:, :width] = tokens_ref[...]
    out_ref[:, width:] = jnp.concatenate(terms, axis=0).T.astype(jnp.bfloat16)


def pack(tokens, routes, gates, helper, home_cap):
    rows, width = tokens.shape
    lanes = 128 * pl.cdiv(3 * helper.shape[0] + 1, 128)
    return pl.pallas_call(
        functools.partial(pack_kernel, home_cap, lanes),
        out_shape=jax.ShapeDtypeStruct((rows, width + lanes), jnp.bfloat16),
        name="pack",
    )(routes.T, gates.T, helper[None, :], tokens)


def expert_kernel(count, experts, *refs):
    token_refs, cot_refs = refs[:count], refs[count : 2 * count]
    sources = refs[2 * count : 2 * count + 6]
    act_ref, grad_ref, held_tokens, held_cot = refs[2 * count + 6 : 2 * count + 10]
    weights, arrived = refs[2 * count + 10 : 2 * count + 16], refs[2 * count + 16]
    rows, width = cot_refs[0].shape
    lanes = token_refs[0].shape[1] - width
    hidden = weights[0].shape[1]
    chip, core, cores = lax.axis_index("expert"), lax.axis_index("dp"), lax.axis_size("dp")
    copies = [
        pltpu.make_async_copy(sources[i], weights[i], arrived.at[i]) for i in range(len(sources))
    ]
    for copy in copies:
        copy.start()
    for i in range(count):
        held_tokens[pl.ds(i * rows, rows), :] = token_refs[i][:, :width]
        held_cot[pl.ds(i * rows, rows), :] = cot_refs[i][...]
    lane = lax.broadcasted_iota(jnp.int32, (rows, lanes), 1)
    grads = []
    for which in range(2):
        gate_w, up_w, down_w = weights[3 * which : 3 * which + 3]
        expert = chip * cores + (core if which == 0 else 1 - core)
        chosen = (lane == expert) | (lane == expert + experts) | (lane == expert + 2 * experts)
        columns = [
            jnp.sum(
                jnp.where(chosen, ref[:, width:].astype(jnp.float32), 0.0), axis=1, keepdims=True
            )
            for ref in token_refs
        ]
        gate = columns[0] if count == 1 else jnp.concatenate(columns, axis=0)
        copies[3 * which].wait()
        gate_pre = jnp.dot(held_tokens[...], gate_w[...], preferred_element_type=jnp.float32)
        copies[3 * which + 1].wait()
        up_pre = jnp.dot(held_tokens[...], up_w[...], preferred_element_type=jnp.float32)
        copies[3 * which + 2].wait()
        back = lax.dot_general(held_cot[...], down_w[...], OVER_LAST, preferred_element_type=jnp.float32)
        sigma = jax.nn.sigmoid(gate_pre)
        active = gate_pre * sigma
        back = back * gate
        grad_up = (back * active).astype(jnp.bfloat16)
        grad_gate = (back * up_pre * sigma * (1.0 + gate_pre * (1.0 - sigma))).astype(jnp.bfloat16)
        scaled_hidden = (active * up_pre * gate).astype(jnp.bfloat16)
        act_ref[:, pl.ds(3 * which * hidden, hidden)] = grad_gate
        act_ref[:, pl.ds((3 * which + 1) * hidden, hidden)] = grad_up
        act_ref[:, pl.ds((3 * which + 2) * hidden, hidden)] = scaled_hidden
        grads += [(grad_gate, gate_w), (grad_up, up_w)]
    step = 512
    for start in range(0, width, step):
        total = None
        for value, weight in grads:
            part = lax.dot_general(
                value, weight[pl.ds(start, step), :], OVER_LAST, preferred_element_type=jnp.float32
            )
            total = part if total is None else total + part
        grad_ref[:, pl.ds(start, step)] = total


def expert_batch(blocks, weights, experts):
    tokens, cots = zip(*blocks)
    rows, width = cots[0].shape
    hidden = weights[0].shape[1]
    total = rows * len(blocks)
    vmem = pl.BlockSpec(memory_space=pltpu.VMEM)
    return pl.pallas_call(
        functools.partial(expert_kernel, len(blocks), experts),
        in_specs=[vmem] * (2 * len(blocks)) + [pl.BlockSpec(memory_space=pl.ANY)] * 6,
        out_specs=[vmem, vmem],
        out_shape=[
            jax.ShapeDtypeStruct((total, 6 * hidden), jnp.bfloat16),
            jax.ShapeDtypeStruct((total, width), jnp.float32),
        ],
        scratch_shapes=[pltpu.VMEM((total, width), jnp.bfloat16)] * 2
        + [pltpu.VMEM(weight.shape, jnp.bfloat16) for weight in weights]
        + [pltpu.SemaphoreType.DMA((6,))],
        compiler_params=pltpu.CompilerParams(vmem_limit_bytes=VMEM_LIMIT),
        cost_estimate=pl.CostEstimate(
            flops=2 * 5 * total * 2 * hidden * width,
            bytes_accessed=12 * hidden * width + total * (8 * width + 12 * hidden),
            transcendentals=2 * total * hidden,
        ),
        name="expert_batch",
    )(*tokens, *cots, *weights)


def row_grads_kernel(counts, add, *refs):
    blocks, batches = counts
    token_refs, act_refs = refs[:blocks], refs[blocks : blocks + batches]
    rest = refs[blocks + batches :]
    terms, (gate_ref, up_ref, acts) = rest[: 2 * add], rest[2 * add :]
    hidden = gate_ref.shape[1]

    @pl.when(pl.program_id(0) == 0)
    def _():
        at = 0
        for ref in act_refs:
            acts[pl.ds(at, ref.shape[0]), :] = ref[:, : 2 * hidden]
            at += ref.shape[0]

    rows = jnp.concatenate([ref[...] for ref in token_refs], axis=0)
    out = lax.dot_general(rows, acts[...], OVER_ROWS, preferred_element_type=jnp.float32)
    for i, ref in enumerate((gate_ref, up_ref)):
        value = out[:, i * hidden : (i + 1) * hidden]
        if add:
            value = value + terms[i][...].astype(jnp.float32)
        ref[...] = value.astype(jnp.bfloat16)


def row_grads(which, tokens, acts, width, terms=()):
    rows = tokens[0].shape[0]
    hidden = acts[0].shape[1] // 6
    total = rows * len(tokens)
    tile = 256
    out_spec = pl.BlockSpec((tile, hidden), lambda j: (j, 0))
    return pl.pallas_call(
        functools.partial(row_grads_kernel, (len(tokens), len(acts)), len(terms) // 2),
        grid=(width // tile,),
        in_specs=[pl.BlockSpec((rows, tile), lambda j: (0, j))] * len(tokens)
        + [pl.BlockSpec((act.shape[0], 3 * hidden), lambda j: (0, which)) for act in acts]
        + [out_spec] * len(terms),
        out_specs=[out_spec] * 2,
        out_shape=[jax.ShapeDtypeStruct((width, hidden), jnp.bfloat16)] * 2,
        scratch_shapes=[pltpu.VMEM((total, 2 * hidden), jnp.bfloat16)],
        compiler_params=pltpu.CompilerParams(vmem_limit_bytes=VMEM_LIMIT),
        cost_estimate=pl.CostEstimate(
            flops=2 * total * width * 2 * hidden,
            bytes_accessed=2 * total * (width + 2 * hidden) + 8 * width * hidden,
            transcendentals=0,
        ),
        name="row_grads",
    )(*tokens, *acts, *terms)


def down_grads_kernel(counts, add, *refs):
    blocks, batches = counts
    cot_refs, act_refs = refs[:blocks], refs[blocks : blocks + batches]
    rest = refs[blocks + batches :]
    terms, (down_ref, acts) = rest[:add], rest[add:]
    hidden = down_ref.shape[0]

    @pl.when(pl.program_id(0) == 0)
    def _():
        at = 0
        for ref in act_refs:
            acts[:, pl.ds(at, ref.shape[0])] = ref[...].T
            at += ref.shape[0]

    rows = jnp.concatenate([ref[...] for ref in cot_refs], axis=0)
    out = jnp.dot(acts[...], rows, preferred_element_type=jnp.float32)
    for term in terms:
        out = out + term[...].astype(jnp.float32)
    down_ref[...] = out.astype(jnp.bfloat16)


def down_grads(which, cots, acts, terms=()):
    rows, width = cots[0].shape
    hidden = acts[0].shape[1] // 6
    total = rows * len(cots)
    tile = 512
    out_spec = pl.BlockSpec((hidden, tile), lambda j: (0, j))
    return pl.pallas_call(
        functools.partial(down_grads_kernel, (len(cots), len(acts)), len(terms)),
        grid=(width // tile,),
        in_specs=[pl.BlockSpec((rows, tile), lambda j: (0, j))] * len(cots)
        + [pl.BlockSpec((act.shape[0], hidden), lambda j: (0, 3 * which + 2)) for act in acts]
        + [out_spec] * len(terms),
        out_specs=out_spec,
        out_shape=jax.ShapeDtypeStruct((hidden, width), jnp.bfloat16),
        scratch_shapes=[pltpu.VMEM((hidden, total), jnp.bfloat16)],
        compiler_params=pltpu.CompilerParams(vmem_limit_bytes=VMEM_LIMIT),
        cost_estimate=pl.CostEstimate(
            flops=2 * total * width * hidden,
            bytes_accessed=2 * total * (width + hidden) + 4 * width * hidden,
            transcendentals=0,
        ),
        name="down_grads",
    )(*cots, *acts, *terms)


def ring_local(ring, tokens, cotangent, routes, gates, helper, w_gate, w_up, w_down):
    rows, width = tokens.shape
    experts = helper.shape[0]
    chips, cores = lax.axis_size("expert"), lax.axis_size("dp")
    route_cap = 2 * rows * routes.shape[1] // (chips * cores)
    home_cap = route_cap - 3 * route_cap // 8
    reach = chips // 2
    up_pairs = [(ring[i], ring[(i + 1) % chips]) for i in range(chips)]
    down_pairs = [(b, a) for a, b in up_pairs]
    swap = [(0, 1), (1, 0)]
    up = lambda value: lax.ppermute(value, "expert", up_pairs)
    down = lambda value: lax.ppermute(value, "expert", down_pairs)
    other = lambda value: lax.ppermute(value, "dp", swap)
    tied = lax.optimization_barrier

    packed = pack(tokens, routes, gates, helper, home_cap)
    own = (w_gate[0], w_up[0], w_down[0])
    weights = own + tuple(other(value) for value in own)
    act, own_grad = expert_batch([(packed, cotangent)], weights, experts)
    row_blocks, cot_blocks, acts = [packed], [cotangent], [act]
    grads_below, grads_above = [], []
    tok_b = tok_a = packed
    cot_b = cot_a = cotangent
    for s in range(1, reach):
        cot_b, cot_a = up(cot_b), down(cot_a)
        tok_b, tok_a = up(tok_b), down(tok_a)
        tok_b, tok_a, acts[-1] = tied((tok_b, tok_a, acts[-1]))
        act, grad = expert_batch(((tok_b, cot_b), (tok_a, cot_a)), weights, experts)
        row_blocks += (tok_b, tok_a)
        cot_blocks += (cot_b, cot_a)
        acts.append(act)
        grads_below.insert(0, grad[:rows])
        grads_above.insert(0, grad[rows:])

    cut = width // 2
    low = lambda value: value[:, :cut]
    high = lambda value: value[:, cut:]
    half = lambda value: value.astype(jnp.bfloat16)
    plus = lambda value, term: half(value.astype(jnp.float32) + term)

    far_cot, far_tok = down(cot_a), up(tok_b)
    high_down, low_up = down(half(high(grads_below[0]))), up(half(low(grads_above[0])))
    far_tok, acts[-1] = tied((far_tok, acts[-1]))
    act, far_grad = expert_batch([(far_tok, far_cot)], weights, experts)
    row_blocks.append(far_tok)
    cot_blocks.append(far_cot)
    acts.append(act)
    low_down, high_up = down(half(low(far_grad))), up(half(high(far_grad)))

    sent, out = {}, {}

    def far_rows():
        parts = row_grads(1, row_blocks, acts, width)
        sent["gate"], sent["up"] = (other(part) for part in parts)
        return parts[0]

    def far_down():
        part = down_grads(1, cot_blocks, acts)
        sent["down"] = other(part)
        return part

    def own_rows():
        terms = (sent["gate"], sent["up"])
        out["gate"], out["up"] = row_grads(0, row_blocks, acts, width, terms)
        return out["gate"]

    def own_down():
        out["down"] = down_grads(0, cot_blocks, acts, (sent["down"],))
        return out["down"]

    chores = [far_rows, far_down, own_rows, own_down]
    for s in range(reach - 1):
        if chores:
            high_down, low_up, _ = tied((high_down, low_up, chores.pop(0)()))
        if s + 1 < reach - 1:
            high_down = down(plus(high_down, high(grads_below[s + 1])))
            low_up = up(plus(low_up, low(grads_above[s + 1])))
        low_down = down(plus(low_down, low(grads_below[s])))
        high_up = up(plus(high_up, high(grads_above[s])))
    for chore in chores:
        chore()

    def three(mine, first, second):
        return half(mine + first.astype(jnp.float32) + second.astype(jnp.float32))

    low_down, high_up, out["down"] = tied((low_down, high_up, out["down"]))
    grad_tokens = jnp.concatenate(
        [three(low(own_grad), low_down, low_up), three(high(own_grad), high_down, high_up)], axis=1
    )
    return (grad_tokens, out["gate"][None], out["up"][None], out["down"][None])


def expert_pass(rows, scaled, gate_w, up_w, down_w):
    gate_pre = jnp.dot(rows, gate_w, preferred_element_type=jnp.float32)
    up_pre = jnp.dot(rows, up_w, preferred_element_type=jnp.float32)
    sigma = jax.nn.sigmoid(gate_pre)
    active = gate_pre * sigma
    hidden = (active * up_pre).astype(jnp.bfloat16)
    over_last = (((1,), (1,)), ((), ()))
    over_rows = (((0,), (0,)), ((), ()))
    back_hidden = lax.dot_general(scaled, down_w, over_last, preferred_element_type=jnp.float32)
    grad_gating = (back_hidden * up_pre * sigma * (1.0 + gate_pre * (1.0 - sigma))).astype(
        jnp.bfloat16
    )
    grad_upward = (back_hidden * active).astype(jnp.bfloat16)
    grad_down = lax.dot_general(hidden, scaled, over_rows, preferred_element_type=jnp.float32)
    grad_gate = lax.dot_general(rows, grad_gating, over_rows, preferred_element_type=jnp.float32)
    grad_up = lax.dot_general(rows, grad_upward, over_rows, preferred_element_type=jnp.float32)
    row_grads = lax.dot_general(grad_gating, gate_w, over_last, preferred_element_type=jnp.float32)
    row_grads = row_grads + lax.dot_general(
        grad_upward, up_w, over_last, preferred_element_type=jnp.float32
    )
    return (row_grads.astype(jnp.bfloat16), grad_gate, grad_up, grad_down)


def exchange_local(tokens, cotangent, routes, gates, helper, w_gate, w_up, w_down):
    tok_rows, width = tokens.shape
    top_count = routes.shape[1]
    devices = lax.axis_size(("expert", "dp"))
    route_cap = 2 * tok_rows * top_count // devices
    spill_cap = 3 * route_cap // 8
    home_cap = route_cap - spill_cap
    block_rows = tok_rows * top_count
    slots = devices * route_cap
    flat_ids = routes.reshape(block_rows)
    experts_row = jnp.arange(devices, dtype=jnp.int32)
    one_hot = (flat_ids[:, None] == experts_row[None, :]).astype(jnp.float32)
    positions = jnp.arange(block_rows, dtype=jnp.int32)
    lower = (positions[:, None] > positions[None, :]).astype(jnp.float32)
    before = jnp.dot(lower, one_hot, precision=lax.Precision.HIGHEST)
    route_rank = jnp.sum(before * one_hot, axis=1).astype(jnp.int32)
    partner_help = helper.reshape(devices // 2, 2)[:, ::-1].reshape(devices).astype(jnp.float32)
    helped = jnp.dot(one_hot, partner_help, precision=lax.Precision.HIGHEST) > 0.5
    spilled = route_rank >= home_cap
    kept = jnp.logical_not(spilled) | helped
    slot_index = jnp.where(kept, flat_ids * route_cap + route_rank, slots)
    source = jnp.full((slots + 1,), block_rows, jnp.int32).at[slot_index].set(positions)[:slots]
    token_of = jnp.where(source < block_rows, source // top_count, tok_rows)
    tokens_pad = jnp.concatenate([tokens, jnp.zeros((1, width), jnp.bfloat16)], axis=0)
    cot_pad = jnp.concatenate([cotangent, jnp.zeros((1, width), jnp.bfloat16)], axis=0)
    gate_pad = jnp.concatenate([gates.reshape(block_rows), jnp.zeros((1,), jnp.float32)], axis=0)
    send_rows = tokens_pad[token_of].reshape(devices, route_cap, width)
    send_scaled = (cot_pad[token_of].astype(jnp.float32) * gate_pad[source][:, None]).astype(
        jnp.bfloat16
    )
    send_scaled = send_scaled.reshape(devices, route_cap, width)
    recv_rows, recv_scaled = (
        lax.all_to_all(send_rows, ("expert", "dp"), split_axis=0, concat_axis=0, tiled=True),
        lax.all_to_all(send_scaled, ("expert", "dp"), split_axis=0, concat_axis=0, tiled=True),
    )
    gate_w = w_gate[0]
    up_w = w_up[0]
    down_w = w_down[0]
    whole_out = expert_pass(
        recv_rows.reshape(slots, width), recv_scaled.reshape(slots, width), gate_w, up_w, down_w
    )
    grad_gate = whole_out[1]
    grad_up = whole_out[2]
    grad_down = whole_out[3]
    row_grads = whole_out[0].reshape(devices, route_cap, width)
    back_rows = lax.all_to_all(row_grads, ("expert", "dp"), split_axis=0, concat_axis=0, tiled=True)
    back_pad = jnp.concatenate(
        [back_rows.reshape(slots, width), jnp.zeros((1, width), jnp.bfloat16)], axis=0
    )
    picked = back_pad[slot_index].reshape(tok_rows, top_count, width)
    grad_tokens = jnp.sum(picked.astype(jnp.float32), axis=1).astype(jnp.bfloat16)
    return (
        grad_tokens,
        grad_gate[None].astype(jnp.bfloat16),
        grad_up[None].astype(jnp.bfloat16),
        grad_down[None].astype(jnp.bfloat16),
    )


def solution(mesh):
    chips, cores = mesh.shape["expert"], mesh.shape["dp"]

    def local(tokens, cotangent, routes, *rest):
        slots = 2 * tokens.shape[0] * routes.shape[1]
        whole = chips * cores * tokens.shape[0]
        if cores == 2 and chips % 2 == 0 and chips > 2 and whole <= 2 * slots:
            return ring_local(ring_of(mesh), tokens, cotangent, routes, *rest)
        return exchange_local(tokens, cotangent, routes, *rest)

    return jax.shard_map(
        local,
        mesh=mesh,
        in_specs=(
            P(("groups", "expert", "dp"), None),
            P(("groups", "expert", "dp"), None),
            P(("groups", "expert", "dp"), None),
            P(("groups", "expert", "dp"), None),
            P("groups"),
            P(("expert", "dp"), None, None),
            P(("expert", "dp"), None, None),
            P(("expert", "dp"), None, None),
        ),
        out_specs=(
            P(("groups", "expert", "dp"), None),
            P(("groups", "expert", "dp"), None, None),
            P(("groups", "expert", "dp"), None, None),
            P(("groups", "expert", "dp"), None, None),
        ),
        check_vma=False,
    )
```

```python
import functools

import jax
import jax.numpy as jnp
from jax import lax
from jax.experimental import pallas as pl
from jax.experimental.pallas import tpu as pltpu
from jax.sharding import PartitionSpec as P

OVER_LAST = (((1,), (1,)), ((), ()))
EXPERT_VMEM = 28 * 1024 * 1024
GRADS_VMEM = 24 * 1024 * 1024
CHEAP = pl.CostEstimate(flops=1024, bytes_accessed=1024, transcendentals=0)


def ring_of(mesh):
    chips = list(mesh.devices[0, :, 0])
    places = [getattr(chip, "coords", None) for chip in chips]
    natural = list(range(len(chips)))
    if any(place is None for place in places):
        return natural
    at = {(place[0], place[2]): i for i, place in enumerate(places)}
    xs = sorted({x for x, _ in at})
    zs = sorted({z for _, z in at})
    if len(at) != len(chips) or len(xs) * len(zs) != len(chips):
        return natural
    if len(xs) == 2:
        return [at[xs[0], z] for z in zs] + [at[xs[1], z] for z in reversed(zs)]
    if len(zs) == 2:
        return [at[x, zs[0]] for x in xs] + [at[x, zs[1]] for x in reversed(xs)]
    return natural


def pack_kernel(home_cap, lanes, routes_ref, gates_ref, helper_ref, tokens_ref, out_ref):
    rows, width = tokens_ref.shape
    experts = helper_ref.shape[1]
    expert_of_row = lax.broadcasted_iota(jnp.int32, (experts, rows), 0)
    named = jnp.zeros((experts, rows), jnp.float32)
    gate = jnp.zeros((experts, rows), jnp.float32)
    for k in range(routes_ref.shape[0]):
        hit = routes_ref[k : k + 1, :] == expert_of_row
        named = named + jnp.where(hit, 1.0, 0.0)
        gate = gate + jnp.where(hit, gates_ref[k : k + 1, :], 0.0)
    earlier = lax.broadcasted_iota(jnp.int32, (rows, rows), 0) < lax.broadcasted_iota(
        jnp.int32, (rows, rows), 1
    )
    rank = jnp.dot(
        named.astype(jnp.bfloat16),
        jnp.where(earlier, 1.0, 0.0).astype(jnp.bfloat16),
        preferred_element_type=jnp.float32,
    )
    partner = jnp.bitwise_xor(lax.broadcasted_iota(jnp.int32, (experts, experts), 0), 1)
    column = lax.broadcasted_iota(jnp.int32, (experts, experts), 1)
    flag = jnp.where(partner == column, helper_ref[...], 0)
    helped = jnp.max(flag, axis=1, keepdims=True) == 1
    gate = jnp.where((rank < home_cap) | helped, gate, 0.0)
    terms = []
    for _ in range(3):
        term = gate.astype(jnp.bfloat16).astype(jnp.float32)
        terms.append(term)
        gate = gate - term
    terms.append(jnp.zeros((lanes - 3 * experts, rows), jnp.float32))
    out_ref[:, :width] = tokens_ref[...]
    out_ref[:, width:] = jnp.concatenate(terms, axis=0).T.astype(jnp.bfloat16)


def pack(tokens, routes, gates, helper, home_cap):
    rows, width = tokens.shape
    lanes = 128 * pl.cdiv(3 * helper.shape[0] + 1, 128)
    return pl.pallas_call(
        functools.partial(pack_kernel, home_cap, lanes),
        out_shape=jax.ShapeDtypeStruct((rows, width + lanes), jnp.bfloat16),
        name="pack",
    )(routes.T, gates.T, helper[None, :], tokens)


def expert_kernel(count, experts, *refs):
    token_refs, cot_refs, sources = refs[:count], refs[count : 2 * count], refs[2 * count : 2 * count + 6]
    rest = refs[2 * count + 6 :]
    outs, rest = rest[: 5 + 2 * count], rest[5 + 2 * count :]
    held_tokens, held_cot, *weights = rest[:8]
    results, (arrived, left) = rest[8:-2], rest[-2:]
    turned, act_refs, hidden_refs, grad_refs = results[0], results[1:3], results[3:5], results[5:]
    rows, width = cot_refs[0].shape
    lanes = token_refs[0].shape[1] - width
    hidden = weights[0].shape[1]
    total = rows * count
    chip, core, cores = lax.axis_index("expert"), lax.axis_index("dp"), lax.axis_size("dp")
    ins = []
    for i in range(count):
        ins.append((token_refs[i], held_tokens.at[pl.ds(i * rows, rows)]))
    ins.append((sources[0], weights[0]))
    ins.append((sources[1], weights[1]))
    for i in range(count):
        ins.append((cot_refs[i], held_cot.at[pl.ds(i * rows, rows)]))
    ins += [(sources[i], weights[i]) for i in range(2, 6)]
    copies = [pltpu.make_async_copy(src, dst, arrived.at[i]) for i, (src, dst) in enumerate(ins)]
    soon = count + 2
    for copy in copies[:soon]:
        copy.start()
    pending = iter(copies)

    def wait(number):
        for _ in range(number):
            next(pending).wait()

    sends = [pltpu.make_async_copy(results[i], outs[i], left.at[i]) for i in range(len(outs))]
    lane = lax.broadcasted_iota(jnp.int32, (total, lanes), 1)
    wait(count)
    gate_terms = held_tokens[:, width:].astype(jnp.float32)
    grads = []
    for which in range(2):
        gate_w, up_w, down_w = weights[3 * which : 3 * which + 3]
        expert = chip * cores + (core if which == 0 else 1 - core)
        chosen = (lane == expert) | (lane == expert + experts) | (lane == expert + 2 * experts)
        gate = jnp.sum(jnp.where(chosen, gate_terms, 0.0), axis=1, keepdims=True)
        rows_in = held_tokens[:, :width]
        wait(1)
        if which == 0:
            for copy in copies[soon:]:
                copy.start()
        gate_pre = jnp.dot(rows_in, gate_w[...], preferred_element_type=jnp.float32)
        wait(1)
        up_pre = jnp.dot(rows_in, up_w[...], preferred_element_type=jnp.float32)
        wait(1 + count if which == 0 else 1)
        back = lax.dot_general(held_cot[...], down_w[...], OVER_LAST, preferred_element_type=jnp.float32)
        sigma = jax.nn.sigmoid(gate_pre)
        active = gate_pre * sigma
        back = back * gate
        grad_up = (back * active).astype(jnp.bfloat16)
        grad_gate = (back * up_pre * sigma * (1.0 + gate_pre * (1.0 - sigma))).astype(jnp.bfloat16)
        scaled_hidden = (active * up_pre * gate).astype(jnp.bfloat16)
        act_refs[which][:, :hidden] = grad_gate
        act_refs[which][:, hidden:] = grad_up
        hidden_refs[which][...] = scaled_hidden.T
        sends[1 + which].start()
        sends[3 + which].start()
        grads += [(grad_gate, gate_w), (grad_up, up_w)]
    step = 512
    cut = width // 2
    for part in range(2):
        for start in range(part * cut, part * cut + cut, step):
            sums = None
            for value, weight in grads:
                term = lax.dot_general(
                    value, weight[pl.ds(start, step), :], OVER_LAST, preferred_element_type=jnp.float32
                )
                sums = term if sums is None else sums + term
            turned[pl.ds(start, step), :] = held_tokens[:, pl.ds(start, step)].T
            for i in range(count):
                ref = grad_refs[2 * i + part]
                ref[:, pl.ds(start - part * cut, step)] = sums[i * rows : (i + 1) * rows].astype(ref.dtype)
        for i in range(count):
            sends[5 + 2 * i + part].start()
    sends[0].start()
    for send in sends:
        send.wait()


def expert_batch(blocks, weights, experts, grad_types):
    tokens, cots = zip(*blocks)
    rows, width = cots[0].shape
    hidden = weights[0].shape[1]
    total = rows * len(blocks)
    anywhere = pl.BlockSpec(memory_space=pl.ANY)
    half = jnp.bfloat16
    results = [((width, total), half)] + [((total, 2 * hidden), half)] * 2 + [((hidden, total), half)] * 2
    results += [((rows, width // 2), kind) for kind in grad_types]
    outs = pl.pallas_call(
        functools.partial(expert_kernel, len(blocks), experts),
        in_specs=[anywhere] * (2 * len(blocks) + 6),
        out_specs=[anywhere] * len(results),
        out_shape=[jax.ShapeDtypeStruct(shape, kind) for shape, kind in results],
        scratch_shapes=[
            pltpu.VMEM((total, tokens[0].shape[1]), half),
            pltpu.VMEM((total, width), half),
        ]
        + [pltpu.VMEM(weight.shape, half) for weight in weights]
        + [pltpu.VMEM(shape, kind) for shape, kind in results]
        + [
            pltpu.SemaphoreType.DMA((2 * len(blocks) + 6,)),
            pltpu.SemaphoreType.DMA((len(results),)),
        ],
        compiler_params=pltpu.CompilerParams(vmem_limit_bytes=EXPERT_VMEM),
        cost_estimate=CHEAP,
        name="expert_batch",
    )(*tokens, *cots, *weights)
    return outs[0], outs[1:3], outs[3:5], outs[5:]


def row_kernel(count, add, *refs):
    turned_refs, act_refs, rest = refs[:count], refs[count : 2 * count], refs[2 * count :]
    terms, outs, held = rest[:add], rest[add:-1], rest[-1]

    @pl.when(pl.program_id(0) == 0)
    def _():
        at = 0
        for ref in act_refs:
            held[pl.ds(at, ref.shape[0]), :] = ref[...]
            at += ref.shape[0]

    tile = jnp.concatenate([ref[...] for ref in turned_refs], axis=1)
    sums = jnp.dot(tile, held[...], preferred_element_type=jnp.float32)
    at = 0
    for i, ref in enumerate(outs):
        value = sums[:, at : at + ref.shape[1]]
        at += ref.shape[1]
        if add:
            value = value + terms[i][...].astype(jnp.float32)
        ref[...] = value.astype(jnp.bfloat16)


def row_grads(turned, acts, terms=()):
    width = turned[0].shape[0]
    hidden = acts[0].shape[1] // 2
    total = sum(act.shape[0] for act in acts)
    tile = 512
    out_spec = pl.BlockSpec((tile, hidden), lambda j: (j, 0))
    return pl.pallas_call(
        functools.partial(row_kernel, len(acts), len(terms)),
        grid=(width // tile,),
        in_specs=[pl.BlockSpec((tile, part.shape[1]), lambda j: (j, 0)) for part in turned]
        + [pl.BlockSpec(act.shape, lambda j: (0, 0)) for act in acts]
        + [out_spec] * len(terms),
        out_specs=[out_spec] * 2,
        out_shape=[jax.ShapeDtypeStruct((width, hidden), jnp.bfloat16)] * 2,
        scratch_shapes=[pltpu.VMEM((total, 2 * hidden), jnp.bfloat16)],
        compiler_params=pltpu.CompilerParams(vmem_limit_bytes=GRADS_VMEM),
        cost_estimate=CHEAP,
        name="row_grads",
    )(*turned, *acts, *terms)


def down_kernel(count, blocks, add, *refs):
    hidden_refs, cot_refs, rest = refs[:count], refs[count : count + blocks], refs[count + blocks :]
    terms, down_ref, held = rest[:add], rest[add], rest[-1]

    @pl.when(pl.program_id(0) == 0)
    def _():
        at = 0
        for ref in hidden_refs:
            held[:, pl.ds(at, ref.shape[1])] = ref[...]
            at += ref.shape[1]

    tile = jnp.concatenate([ref[...] for ref in cot_refs], axis=0)
    sums = jnp.dot(held[...], tile, preferred_element_type=jnp.float32)
    for term in terms:
        sums = sums + term[...].astype(jnp.float32)
    down_ref[...] = sums.astype(jnp.bfloat16)


def down_grads(hiddens, cots, terms=()):
    rows, width = cots[0].shape
    hidden = hiddens[0].shape[0]
    total = rows * len(cots)
    tile = 512
    out_spec = pl.BlockSpec((hidden, tile), lambda j: (0, j))
    return pl.pallas_call(
        functools.partial(down_kernel, len(hiddens), len(cots), len(terms)),
        grid=(width // tile,),
        in_specs=[pl.BlockSpec(part.shape, lambda j: (0, 0)) for part in hiddens]
        + [pl.BlockSpec((rows, tile), lambda j: (0, j))] * len(cots)
        + [out_spec] * len(terms),
        out_specs=out_spec,
        out_shape=jax.ShapeDtypeStruct((hidden, width), jnp.bfloat16),
        scratch_shapes=[pltpu.VMEM((hidden, total), jnp.bfloat16)],
        compiler_params=pltpu.CompilerParams(vmem_limit_bytes=GRADS_VMEM),
        cost_estimate=CHEAP,
        name="down_grads",
    )(*hiddens, *cots, *terms)


def ring_local(ring, tokens, cotangent, routes, gates, helper, w_gate, w_up, w_down):
    experts = helper.shape[0]
    chips, cores = lax.axis_size("expert"), lax.axis_size("dp")
    route_cap = 2 * tokens.shape[0] * routes.shape[1] // (chips * cores)
    home_cap = route_cap - 3 * route_cap // 8
    reach = chips // 2
    up_pairs = [(ring[i], ring[(i + 1) % chips]) for i in range(chips)]
    down_pairs = [(b, a) for a, b in up_pairs]
    swap = [(0, 1), (1, 0)]
    up = lambda value: lax.ppermute(value, "expert", up_pairs)
    down = lambda value: lax.ppermute(value, "expert", down_pairs)
    other = lambda value: lax.ppermute(value, "dp", swap)
    tied = lax.optimization_barrier
    wide, half = jnp.float32, jnp.bfloat16

    packed = pack(tokens, routes, gates, helper, home_cap)
    packed, own = tied((packed, (w_gate[0], w_up[0], w_down[0])))
    weights = own + tuple(other(value) for value in own)
    turned, acts, hiddens, cots = [], [], [], []

    def batch(blocks, grad_types):
        turn, act, hid, grads = expert_batch(blocks, weights, experts, grad_types)
        turned.append(turn)
        acts.append(act)
        hiddens.append(hid)
        cots.extend(cot for _, cot in blocks)
        return grads

    own_low, own_high = batch([(packed, cotangent)], (wide, wide))
    below_low, below_high, above_low, above_high = [], [], [], []
    tok_b = tok_a = packed
    cot_b = cot_a = cotangent
    for s in range(1, reach):
        cot_b, cot_a = up(cot_b), down(cot_a)
        tok_b, tok_a = up(tok_b), down(tok_a)
        tok_b, tok_a, turned[-1] = tied((tok_b, tok_a, turned[-1]))
        last = half if s == reach - 1 else wide
        parts = batch([(tok_b, cot_b), (tok_a, cot_a)], (wide, last, last, wide))
        for store, part in zip((below_low, below_high, above_low, above_high), parts):
            store.insert(0, part)

    plus = lambda value, term: (value.astype(wide) + term).astype(half)
    far_cot, far_tok = down(cot_a), up(tok_b)
    high_down, low_up = down(below_high[0]), up(above_low[0])
    far_tok, turned[-1] = tied((far_tok, turned[-1]))
    far_low, far_high = batch([(far_tok, far_cot)], (half, half))
    low_down, high_up = down(far_low), up(far_high)

    sent, out = {}, {}

    def far_rows():
        parts = row_grads(turned, [act[1] for act in acts])
        sent["gate"], sent["up"] = (other(part) for part in parts)
        return parts[0]

    def far_down():
        part = down_grads([hid[1] for hid in hiddens], cots)
        sent["down"] = other(part)
        return part

    def own_rows():
        terms = (sent["gate"], sent["up"])
        out["gate"], out["up"] = row_grads(turned, [act[0] for act in acts], terms)
        return out["gate"]

    def own_down():
        out["down"] = down_grads([hid[0] for hid in hiddens], cots, (sent["down"],))
        return out["down"]

    chores = [far_rows, far_down, own_rows, own_down]

    def before_chore(first, second):
        first, second, turned[-1], cots[-1] = tied((first, second, turned[-1], cots[-1]))
        return first, second

    def after_chore(first, second):
        first, second, _ = tied((first, second, chores.pop(0)()))
        return first, second

    for s in range(reach - 1):
        if s + 1 < reach - 1:
            high_down, low_up = plus(high_down, below_high[s + 1]), plus(low_up, above_low[s + 1])
            high_down, low_up = before_chore(high_down, low_up)
            high_down, low_up = down(high_down), up(low_up)
        if s != 1 and chores:
            low_down, high_up = after_chore(low_down, high_up)
        low_down, high_up = plus(low_down, below_low[s]), plus(high_up, above_high[s])
        low_down, high_up = before_chore(low_down, high_up)
        low_down, high_up = down(low_down), up(high_up)
        if s == 0 and chores:
            high_down, low_up = after_chore(high_down, low_up)
    while chores:
        low_down, high_up = after_chore(low_down, high_up)

    grad_low = (own_low + low_down.astype(wide) + low_up.astype(wide)).astype(half)
    grad_high = (own_high + high_down.astype(wide) + high_up.astype(wide)).astype(half)
    grad_tokens = jnp.concatenate([grad_low, grad_high], axis=1)
    return (grad_tokens, out["gate"][None], out["up"][None], out["down"][None])


def expert_pass(rows, scaled, gate_w, up_w, down_w):
    gate_pre = jnp.dot(rows, gate_w, preferred_element_type=jnp.float32)
    up_pre = jnp.dot(rows, up_w, preferred_element_type=jnp.float32)
    sigma = jax.nn.sigmoid(gate_pre)
    active = gate_pre * sigma
    hidden = (active * up_pre).astype(jnp.bfloat16)
    over_last = (((1,), (1,)), ((), ()))
    over_rows = (((0,), (0,)), ((), ()))
    back_hidden = lax.dot_general(scaled, down_w, over_last, preferred_element_type=jnp.float32)
    grad_gating = (back_hidden * up_pre * sigma * (1.0 + gate_pre * (1.0 - sigma))).astype(
        jnp.bfloat16
    )
    grad_upward = (back_hidden * active).astype(jnp.bfloat16)
    grad_down = lax.dot_general(hidden, scaled, over_rows, preferred_element_type=jnp.float32)
    grad_gate = lax.dot_general(rows, grad_gating, over_rows, preferred_element_type=jnp.float32)
    grad_up = lax.dot_general(rows, grad_upward, over_rows, preferred_element_type=jnp.float32)
    row_grads = lax.dot_general(grad_gating, gate_w, over_last, preferred_element_type=jnp.float32)
    row_grads = row_grads + lax.dot_general(
        grad_upward, up_w, over_last, preferred_element_type=jnp.float32
    )
    return (row_grads.astype(jnp.bfloat16), grad_gate, grad_up, grad_down)


def exchange_local(tokens, cotangent, routes, gates, helper, w_gate, w_up, w_down):
    tok_rows, width = tokens.shape
    top_count = routes.shape[1]
    devices = lax.axis_size(("expert", "dp"))
    route_cap = 2 * tok_rows * top_count // devices
    spill_cap = 3 * route_cap // 8
    home_cap = route_cap - spill_cap
    block_rows = tok_rows * top_count
    slots = devices * route_cap
    flat_ids = routes.reshape(block_rows)
    experts_row = jnp.arange(devices, dtype=jnp.int32)
    one_hot = (flat_ids[:, None] == experts_row[None, :]).astype(jnp.float32)
    positions = jnp.arange(block_rows, dtype=jnp.int32)
    lower = (positions[:, None] > positions[None, :]).astype(jnp.float32)
    before = jnp.dot(lower, one_hot, precision=lax.Precision.HIGHEST)
    route_rank = jnp.sum(before * one_hot, axis=1).astype(jnp.int32)
    partner_help = helper.reshape(devices // 2, 2)[:, ::-1].reshape(devices).astype(jnp.float32)
    helped = jnp.dot(one_hot, partner_help, precision=lax.Precision.HIGHEST) > 0.5
    spilled = route_rank >= home_cap
    kept = jnp.logical_not(spilled) | helped
    slot_index = jnp.where(kept, flat_ids * route_cap + route_rank, slots)
    source = jnp.full((slots + 1,), block_rows, jnp.int32).at[slot_index].set(positions)[:slots]
    token_of = jnp.where(source < block_rows, source // top_count, tok_rows)
    tokens_pad = jnp.concatenate([tokens, jnp.zeros((1, width), jnp.bfloat16)], axis=0)
    cot_pad = jnp.concatenate([cotangent, jnp.zeros((1, width), jnp.bfloat16)], axis=0)
    gate_pad = jnp.concatenate([gates.reshape(block_rows), jnp.zeros((1,), jnp.float32)], axis=0)
    send_rows = tokens_pad[token_of].reshape(devices, route_cap, width)
    send_scaled = (cot_pad[token_of].astype(jnp.float32) * gate_pad[source][:, None]).astype(
        jnp.bfloat16
    )
    send_scaled = send_scaled.reshape(devices, route_cap, width)
    recv_rows, recv_scaled = (
        lax.all_to_all(send_rows, ("expert", "dp"), split_axis=0, concat_axis=0, tiled=True),
        lax.all_to_all(send_scaled, ("expert", "dp"), split_axis=0, concat_axis=0, tiled=True),
    )
    gate_w = w_gate[0]
    up_w = w_up[0]
    down_w = w_down[0]
    whole_out = expert_pass(
        recv_rows.reshape(slots, width), recv_scaled.reshape(slots, width), gate_w, up_w, down_w
    )
    grad_gate = whole_out[1]
    grad_up = whole_out[2]
    grad_down = whole_out[3]
    row_grads = whole_out[0].reshape(devices, route_cap, width)
    back_rows = lax.all_to_all(row_grads, ("expert", "dp"), split_axis=0, concat_axis=0, tiled=True)
    back_pad = jnp.concatenate(
        [back_rows.reshape(slots, width), jnp.zeros((1, width), jnp.bfloat16)], axis=0
    )
    picked = back_pad[slot_index].reshape(tok_rows, top_count, width)
    grad_tokens = jnp.sum(picked.astype(jnp.float32), axis=1).astype(jnp.bfloat16)
    return (
        grad_tokens,
        grad_gate[None].astype(jnp.bfloat16),
        grad_up[None].astype(jnp.bfloat16),
        grad_down[None].astype(jnp.bfloat16),
    )


def solution(mesh):
    chips, cores = mesh.shape["expert"], mesh.shape["dp"]

    def local(tokens, cotangent, routes, *rest):
        slots = 2 * tokens.shape[0] * routes.shape[1]
        whole = chips * cores * tokens.shape[0]
        if cores == 2 and chips % 2 == 0 and chips > 2 and whole <= 2 * slots:
            return ring_local(ring_of(mesh), tokens, cotangent, routes, *rest)
        return exchange_local(tokens, cotangent, routes, *rest)

    return jax.shard_map(
        local,
        mesh=mesh,
        in_specs=(
            P(("groups", "expert", "dp"), None),
            P(("groups", "expert", "dp"), None),
            P(("groups", "expert", "dp"), None),
            P(("groups", "expert", "dp"), None),
            P("groups"),
            P(("expert", "dp"), None, None),
            P(("expert", "dp"), None, None),
            P(("expert", "dp"), None, None),
        ),
        out_specs=(
            P(("groups", "expert", "dp"), None),
            P(("groups", "expert", "dp"), None, None),
            P(("groups", "expert", "dp"), None, None),
            P(("groups", "expert", "dp"), None, None),
        ),
        check_vma=False,
    )
```

```python
import functools

import jax
import jax.numpy as jnp
from jax import lax
from jax.experimental import pallas as pl
from jax.experimental.pallas import tpu as pltpu
from jax.sharding import PartitionSpec as P

OVER_LAST = (((1,), (1,)), ((), ()))
EXPERT_VMEM = 28 * 1024 * 1024
GRADS_VMEM = 24 * 1024 * 1024
CHEAP = pl.CostEstimate(flops=1024, bytes_accessed=1024, transcendentals=0)


def ring_of(mesh):
    chips = list(mesh.devices[0, :, 0])
    places = [getattr(chip, "coords", None) for chip in chips]
    natural = list(range(len(chips)))
    if any(place is None for place in places):
        return natural
    at = {(place[0], place[2]): i for i, place in enumerate(places)}
    xs = sorted({x for x, _ in at})
    zs = sorted({z for _, z in at})
    if len(at) != len(chips) or len(xs) * len(zs) != len(chips):
        return natural
    if len(xs) == 2:
        return [at[xs[0], z] for z in zs] + [at[xs[1], z] for z in reversed(zs)]
    if len(zs) == 2:
        return [at[x, zs[0]] for x in xs] + [at[x, zs[1]] for x in reversed(xs)]
    return natural


def pack_kernel(home_cap, lanes, routes_ref, gates_ref, helper_ref, tokens_ref, out_ref):
    rows, width = tokens_ref.shape
    experts = helper_ref.shape[1]
    expert_of_row = lax.broadcasted_iota(jnp.int32, (experts, rows), 0)
    named = jnp.zeros((experts, rows), jnp.float32)
    gate = jnp.zeros((experts, rows), jnp.float32)
    for k in range(routes_ref.shape[0]):
        hit = routes_ref[k : k + 1, :] == expert_of_row
        named = named + jnp.where(hit, 1.0, 0.0)
        gate = gate + jnp.where(hit, gates_ref[k : k + 1, :], 0.0)
    earlier = lax.broadcasted_iota(jnp.int32, (rows, rows), 0) < lax.broadcasted_iota(
        jnp.int32, (rows, rows), 1
    )
    rank = jnp.dot(
        named.astype(jnp.bfloat16),
        jnp.where(earlier, 1.0, 0.0).astype(jnp.bfloat16),
        preferred_element_type=jnp.float32,
    )
    partner = jnp.bitwise_xor(lax.broadcasted_iota(jnp.int32, (experts, experts), 0), 1)
    column = lax.broadcasted_iota(jnp.int32, (experts, experts), 1)
    flag = jnp.where(partner == column, helper_ref[...], 0)
    helped = jnp.max(flag, axis=1, keepdims=True) == 1
    gate = jnp.where((rank < home_cap) | helped, gate, 0.0)
    terms = []
    for _ in range(3):
        term = gate.astype(jnp.bfloat16).astype(jnp.float32)
        terms.append(term)
        gate = gate - term
    terms.append(jnp.zeros((lanes - 3 * experts, rows), jnp.float32))
    out_ref[:, :width] = tokens_ref[...]
    out_ref[:, width:] = jnp.concatenate(terms, axis=0).T.astype(jnp.bfloat16)


def pack(tokens, routes, gates, helper, home_cap):
    rows, width = tokens.shape
    lanes = 128 * pl.cdiv(3 * helper.shape[0] + 1, 128)
    return pl.pallas_call(
        functools.partial(pack_kernel, home_cap, lanes),
        out_shape=jax.ShapeDtypeStruct((rows, width + lanes), jnp.bfloat16),
        name="pack",
    )(routes.T, gates.T, helper[None, :], tokens)


def expert_kernel(count, experts, *refs):
    token_refs, cot_refs, sources = refs[:count], refs[count : 2 * count], refs[2 * count : 2 * count + 6]
    rest = refs[2 * count + 6 :]
    outs, rest = rest[: 5 + 2 * count], rest[5 + 2 * count :]
    held_tokens, held_cot, *weights = rest[:8]
    results, (arrived, left) = rest[8:-2], rest[-2:]
    turned, act_refs, hidden_refs, grad_refs = results[0], results[1:3], results[3:5], results[5:]
    rows, width = cot_refs[0].shape
    lanes = token_refs[0].shape[1] - width
    hidden = weights[0].shape[1]
    total = rows * count
    chip, core, cores = lax.axis_index("expert"), lax.axis_index("dp"), lax.axis_size("dp")
    ins = []
    for i in range(count):
        ins.append((token_refs[i], held_tokens.at[pl.ds(i * rows, rows)]))
    ins.append((sources[0], weights[0]))
    ins.append((sources[1], weights[1]))
    for i in range(count):
        ins.append((cot_refs[i], held_cot.at[pl.ds(i * rows, rows)]))
    ins += [(sources[i], weights[i]) for i in range(2, 6)]
    copies = [pltpu.make_async_copy(src, dst, arrived.at[i]) for i, (src, dst) in enumerate(ins)]
    soon = count + 2
    for copy in copies[:soon]:
        copy.start()
    pending = iter(copies)

    def wait(number):
        for _ in range(number):
            next(pending).wait()

    sends = [pltpu.make_async_copy(results[i], outs[i], left.at[i]) for i in range(len(outs))]
    lane = lax.broadcasted_iota(jnp.int32, (total, lanes), 1)
    wait(count)
    gate_terms = held_tokens[:, width:].astype(jnp.float32)
    grads = []
    for which in range(2):
        gate_w, up_w, down_w = weights[3 * which : 3 * which + 3]
        expert = chip * cores + (core if which == 0 else 1 - core)
        chosen = (lane == expert) | (lane == expert + experts) | (lane == expert + 2 * experts)
        gate = jnp.sum(jnp.where(chosen, gate_terms, 0.0), axis=1, keepdims=True)
        rows_in = held_tokens[:, :width]
        wait(1)
        if which == 0:
            for copy in copies[soon:]:
                copy.start()
        gate_pre = jnp.dot(rows_in, gate_w[...], preferred_element_type=jnp.float32)
        wait(1)
        up_pre = jnp.dot(rows_in, up_w[...], preferred_element_type=jnp.float32)
        wait(1 + count if which == 0 else 1)
        back = lax.dot_general(held_cot[...], down_w[...], OVER_LAST, preferred_element_type=jnp.float32)
        sigma = jax.nn.sigmoid(gate_pre)
        active = gate_pre * sigma
        back = back * gate
        grad_up = (back * active).astype(jnp.bfloat16)
        grad_gate = (back * up_pre * sigma * (1.0 + gate_pre * (1.0 - sigma))).astype(jnp.bfloat16)
        scaled_hidden = (active * up_pre * gate).astype(jnp.bfloat16)
        act_refs[which][:, :hidden] = grad_gate
        act_refs[which][:, hidden:] = grad_up
        hidden_refs[which][...] = scaled_hidden.T
        sends[1 + which].start()
        sends[3 + which].start()
        grads += [(grad_gate, gate_w), (grad_up, up_w)]
    step = 512
    cut = width // 2
    for part in range(2):
        for start in range(part * cut, part * cut + cut, step):
            sums = None
            for value, weight in grads:
                term = lax.dot_general(
                    value, weight[pl.ds(start, step), :], OVER_LAST, preferred_element_type=jnp.float32
                )
                sums = term if sums is None else sums + term
            turned[pl.ds(start, step), :] = held_tokens[:, pl.ds(start, step)].T
            for i in range(count):
                ref = grad_refs[2 * i + part]
                ref[:, pl.ds(start - part * cut, step)] = sums[i * rows : (i + 1) * rows].astype(ref.dtype)
        for i in range(count):
            sends[5 + 2 * i + part].start()
    sends[0].start()
    for send in sends:
        send.wait()


def expert_batch(blocks, weights, experts, grad_types):
    tokens, cots = zip(*blocks)
    rows, width = cots[0].shape
    hidden = weights[0].shape[1]
    total = rows * len(blocks)
    anywhere = pl.BlockSpec(memory_space=pl.ANY)
    half = jnp.bfloat16
    results = [((width, total), half)] + [((total, 2 * hidden), half)] * 2 + [((hidden, total), half)] * 2
    results += [((rows, width // 2), kind) for kind in grad_types]
    outs = pl.pallas_call(
        functools.partial(expert_kernel, len(blocks), experts),
        in_specs=[anywhere] * (2 * len(blocks) + 6),
        out_specs=[anywhere] * len(results),
        out_shape=[jax.ShapeDtypeStruct(shape, kind) for shape, kind in results],
        scratch_shapes=[
            pltpu.VMEM((total, tokens[0].shape[1]), half),
            pltpu.VMEM((total, width), half),
        ]
        + [pltpu.VMEM(weight.shape, half) for weight in weights]
        + [pltpu.VMEM(shape, kind) for shape, kind in results]
        + [
            pltpu.SemaphoreType.DMA((2 * len(blocks) + 6,)),
            pltpu.SemaphoreType.DMA((len(results),)),
        ],
        compiler_params=pltpu.CompilerParams(vmem_limit_bytes=EXPERT_VMEM),
        cost_estimate=CHEAP,
        name="expert_batch",
    )(*tokens, *cots, *weights)
    return outs[0], outs[1:3], outs[3:5], outs[5:]


def row_kernel(count, add, *refs):
    turned_refs, act_refs, rest = refs[:count], refs[count : 2 * count], refs[2 * count :]
    terms, outs, held = rest[:add], rest[add:-1], rest[-1]

    @pl.when(pl.program_id(0) == 0)
    def _():
        at = 0
        for ref in act_refs:
            held[pl.ds(at, ref.shape[0]), :] = ref[...]
            at += ref.shape[0]

    tile = jnp.concatenate([ref[...] for ref in turned_refs], axis=1)
    sums = jnp.dot(tile, held[...], preferred_element_type=jnp.float32)
    at = 0
    for i, ref in enumerate(outs):
        value = sums[:, at : at + ref.shape[1]]
        at += ref.shape[1]
        if add:
            value = value + terms[i][...].astype(jnp.float32)
        ref[...] = value.astype(jnp.bfloat16)


def row_grads(turned, acts, terms=()):
    width = turned[0].shape[0]
    hidden = acts[0].shape[1] // 2
    total = sum(act.shape[0] for act in acts)
    tile = 512
    out_spec = pl.BlockSpec((tile, hidden), lambda j: (j, 0))
    return pl.pallas_call(
        functools.partial(row_kernel, len(acts), len(terms)),
        grid=(width // tile,),
        in_specs=[pl.BlockSpec((tile, part.shape[1]), lambda j: (j, 0)) for part in turned]
        + [pl.BlockSpec(act.shape, lambda j: (0, 0)) for act in acts]
        + [out_spec] * len(terms),
        out_specs=[out_spec] * 2,
        out_shape=[jax.ShapeDtypeStruct((width, hidden), jnp.bfloat16)] * 2,
        scratch_shapes=[pltpu.VMEM((total, 2 * hidden), jnp.bfloat16)],
        compiler_params=pltpu.CompilerParams(vmem_limit_bytes=GRADS_VMEM),
        cost_estimate=CHEAP,
        name="row_grads",
    )(*turned, *acts, *terms)


def down_kernel(count, blocks, add, *refs):
    hidden_refs, cot_refs, rest = refs[:count], refs[count : count + blocks], refs[count + blocks :]
    terms, down_ref, held = rest[:add], rest[add], rest[-1]

    @pl.when(pl.program_id(0) == 0)
    def _():
        at = 0
        for ref in hidden_refs:
            held[:, pl.ds(at, ref.shape[1])] = ref[...]
            at += ref.shape[1]

    tile = jnp.concatenate([ref[...] for ref in cot_refs], axis=0)
    sums = jnp.dot(held[...], tile, preferred_element_type=jnp.float32)
    for term in terms:
        sums = sums + term[...].astype(jnp.float32)
    down_ref[...] = sums.astype(jnp.bfloat16)


def down_grads(hiddens, cots, terms=()):
    rows, width = cots[0].shape
    hidden = hiddens[0].shape[0]
    total = rows * len(cots)
    tile = 512
    out_spec = pl.BlockSpec((hidden, tile), lambda j: (0, j))
    return pl.pallas_call(
        functools.partial(down_kernel, len(hiddens), len(cots), len(terms)),
        grid=(width // tile,),
        in_specs=[pl.BlockSpec(part.shape, lambda j: (0, 0)) for part in hiddens]
        + [pl.BlockSpec((rows, tile), lambda j: (0, j))] * len(cots)
        + [out_spec] * len(terms),
        out_specs=out_spec,
        out_shape=jax.ShapeDtypeStruct((hidden, width), jnp.bfloat16),
        scratch_shapes=[pltpu.VMEM((hidden, total), jnp.bfloat16)],
        compiler_params=pltpu.CompilerParams(vmem_limit_bytes=GRADS_VMEM),
        cost_estimate=CHEAP,
        name="down_grads",
    )(*hiddens, *cots, *terms)


def ring_local(ring, tokens, cotangent, routes, gates, helper, w_gate, w_up, w_down):
    experts = helper.shape[0]
    chips, cores = lax.axis_size("expert"), lax.axis_size("dp")
    route_cap = 2 * tokens.shape[0] * routes.shape[1] // (chips * cores)
    home_cap = route_cap - 3 * route_cap // 8
    reach = chips // 2
    up_pairs = [(ring[i], ring[(i + 1) % chips]) for i in range(chips)]
    down_pairs = [(b, a) for a, b in up_pairs]
    swap = [(0, 1), (1, 0)]
    up = lambda value: lax.ppermute(value, "expert", up_pairs)
    down = lambda value: lax.ppermute(value, "expert", down_pairs)
    other = lambda value: lax.ppermute(value, "dp", swap)
    tied = lax.optimization_barrier
    wide, half = jnp.float32, jnp.bfloat16

    packed = pack(tokens, routes, gates, helper, home_cap)
    packed, own = tied((packed, (w_gate[0], w_up[0], w_down[0])))
    weights = own + tuple(other(value) for value in own)
    turned, acts, hiddens, cots = [], [], [], []

    def batch(blocks, grad_types):
        turn, act, hid, grads = expert_batch(blocks, weights, experts, grad_types)
        turned.append(turn)
        acts.append(act)
        hiddens.append(hid)
        cots.extend(cot for _, cot in blocks)
        return grads

    own_low, own_high = batch([(packed, cotangent)], (wide, wide))
    below_low, below_high, above_low, above_high = [], [], [], []
    tok_b = tok_a = packed
    cot_b = cot_a = cotangent
    for s in range(1, reach):
        cot_b, cot_a = up(cot_b), down(cot_a)
        tok_b, tok_a = up(tok_b), down(tok_a)
        tok_b, tok_a, turned[-1] = tied((tok_b, tok_a, turned[-1]))
        last = half if s == reach - 1 else wide
        parts = batch([(tok_b, cot_b), (tok_a, cot_a)], (wide, last, last, wide))
        for store, part in zip((below_low, below_high, above_low, above_high), parts):
            store.insert(0, part)

    plus = lambda value, term: (value.astype(wide) + term).astype(half)
    far_cot, far_tok = down(cot_a), up(tok_b)
    high_down, low_up = down(below_high[0]), up(above_low[0])
    far_tok, turned[-1] = tied((far_tok, turned[-1]))
    far_low, far_high = batch([(far_tok, far_cot)], (half, half))
    low_down, high_up = down(far_low), up(far_high)

    sent, out = {}, {}

    def far_rows():
        parts = row_grads(turned, [act[1] for act in acts])
        sent["gate"], sent["up"] = (other(part) for part in parts)
        return parts[0]

    def far_down():
        part = down_grads([hid[1] for hid in hiddens], cots)
        sent["down"] = other(part)
        return part

    def own_rows():
        terms = (sent["gate"], sent["up"])
        out["gate"], out["up"] = row_grads(turned, [act[0] for act in acts], terms)
        return out["gate"]

    def own_down():
        out["down"] = down_grads([hid[0] for hid in hiddens], cots, (sent["down"],))
        return out["down"]

    chores = [far_rows, far_down, own_rows, own_down]

    def before_chore(first, second):
        first, second, turned[-1], cots[-1] = tied((first, second, turned[-1], cots[-1]))
        return first, second

    def after_chore(first, second):
        first, second, _ = tied((first, second, chores.pop(0)()))
        return first, second

    for s in range(reach - 1):
        more = s + 1 < reach - 1
        if more:
            high_down, low_up = plus(high_down, below_high[s + 1]), plus(low_up, above_low[s + 1])
            high_down, low_up = before_chore(high_down, low_up)
            high_down, low_up = down(high_down), up(low_up)
        if s > 0 and more and chores:
            high_down, low_up = after_chore(high_down, low_up)
            low_down, high_up, high_down, low_up = tied((low_down, high_up, high_down, low_up))
        elif chores:
            low_down, high_up = after_chore(low_down, high_up)
        low_down, high_up = plus(low_down, below_low[s]), plus(high_up, above_high[s])
        low_down, high_up = before_chore(low_down, high_up)
        low_down, high_up = down(low_down), up(high_up)
    while chores:
        low_down, high_up = after_chore(low_down, high_up)

    grad_low = (own_low + low_down.astype(wide) + low_up.astype(wide)).astype(half)
    grad_high = (own_high + high_down.astype(wide) + high_up.astype(wide)).astype(half)
    grad_tokens = jnp.concatenate([grad_low, grad_high], axis=1)
    return (grad_tokens, out["gate"][None], out["up"][None], out["down"][None])


def expert_pass(rows, scaled, gate_w, up_w, down_w):
    gate_pre = jnp.dot(rows, gate_w, preferred_element_type=jnp.float32)
    up_pre = jnp.dot(rows, up_w, preferred_element_type=jnp.float32)
    sigma = jax.nn.sigmoid(gate_pre)
    active = gate_pre * sigma
    hidden = (active * up_pre).astype(jnp.bfloat16)
    over_last = (((1,), (1,)), ((), ()))
    over_rows = (((0,), (0,)), ((), ()))
    back_hidden = lax.dot_general(scaled, down_w, over_last, preferred_element_type=jnp.float32)
    grad_gating = (back_hidden * up_pre * sigma * (1.0 + gate_pre * (1.0 - sigma))).astype(
        jnp.bfloat16
    )
    grad_upward = (back_hidden * active).astype(jnp.bfloat16)
    grad_down = lax.dot_general(hidden, scaled, over_rows, preferred_element_type=jnp.float32)
    grad_gate = lax.dot_general(rows, grad_gating, over_rows, preferred_element_type=jnp.float32)
    grad_up = lax.dot_general(rows, grad_upward, over_rows, preferred_element_type=jnp.float32)
    row_grads = lax.dot_general(grad_gating, gate_w, over_last, preferred_element_type=jnp.float32)
    row_grads = row_grads + lax.dot_general(
        grad_upward, up_w, over_last, preferred_element_type=jnp.float32
    )
    return (row_grads.astype(jnp.bfloat16), grad_gate, grad_up, grad_down)


def exchange_local(tokens, cotangent, routes, gates, helper, w_gate, w_up, w_down):
    tok_rows, width = tokens.shape
    top_count = routes.shape[1]
    devices = lax.axis_size(("expert", "dp"))
    route_cap = 2 * tok_rows * top_count // devices
    spill_cap = 3 * route_cap // 8
    home_cap = route_cap - spill_cap
    block_rows = tok_rows * top_count
    slots = devices * route_cap
    flat_ids = routes.reshape(block_rows)
    experts_row = jnp.arange(devices, dtype=jnp.int32)
    one_hot = (flat_ids[:, None] == experts_row[None, :]).astype(jnp.float32)
    positions = jnp.arange(block_rows, dtype=jnp.int32)
    lower = (positions[:, None] > positions[None, :]).astype(jnp.float32)
    before = jnp.dot(lower, one_hot, precision=lax.Precision.HIGHEST)
    route_rank = jnp.sum(before * one_hot, axis=1).astype(jnp.int32)
    partner_help = helper.reshape(devices // 2, 2)[:, ::-1].reshape(devices).astype(jnp.float32)
    helped = jnp.dot(one_hot, partner_help, precision=lax.Precision.HIGHEST) > 0.5
    spilled = route_rank >= home_cap
    kept = jnp.logical_not(spilled) | helped
    slot_index = jnp.where(kept, flat_ids * route_cap + route_rank, slots)
    source = jnp.full((slots + 1,), block_rows, jnp.int32).at[slot_index].set(positions)[:slots]
    token_of = jnp.where(source < block_rows, source // top_count, tok_rows)
    tokens_pad = jnp.concatenate([tokens, jnp.zeros((1, width), jnp.bfloat16)], axis=0)
    cot_pad = jnp.concatenate([cotangent, jnp.zeros((1, width), jnp.bfloat16)], axis=0)
    gate_pad = jnp.concatenate([gates.reshape(block_rows), jnp.zeros((1,), jnp.float32)], axis=0)
    send_rows = tokens_pad[token_of].reshape(devices, route_cap, width)
    send_scaled = (cot_pad[token_of].astype(jnp.float32) * gate_pad[source][:, None]).astype(
        jnp.bfloat16
    )
    send_scaled = send_scaled.reshape(devices, route_cap, width)
    recv_rows, recv_scaled = (
        lax.all_to_all(send_rows, ("expert", "dp"), split_axis=0, concat_axis=0, tiled=True),
        lax.all_to_all(send_scaled, ("expert", "dp"), split_axis=0, concat_axis=0, tiled=True),
    )
    gate_w = w_gate[0]
    up_w = w_up[0]
    down_w = w_down[0]
    whole_out = expert_pass(
        recv_rows.reshape(slots, width), recv_scaled.reshape(slots, width), gate_w, up_w, down_w
    )
    grad_gate = whole_out[1]
    grad_up = whole_out[2]
    grad_down = whole_out[3]
    row_grads = whole_out[0].reshape(devices, route_cap, width)
    back_rows = lax.all_to_all(row_grads, ("expert", "dp"), split_axis=0, concat_axis=0, tiled=True)
    back_pad = jnp.concatenate(
        [back_rows.reshape(slots, width), jnp.zeros((1, width), jnp.bfloat16)], axis=0
    )
    picked = back_pad[slot_index].reshape(tok_rows, top_count, width)
    grad_tokens = jnp.sum(picked.astype(jnp.float32), axis=1).astype(jnp.bfloat16)
    return (
        grad_tokens,
        grad_gate[None].astype(jnp.bfloat16),
        grad_up[None].astype(jnp.bfloat16),
        grad_down[None].astype(jnp.bfloat16),
    )


def solution(mesh):
    chips, cores = mesh.shape["expert"], mesh.shape["dp"]

    def local(tokens, cotangent, routes, *rest):
        slots = 2 * tokens.shape[0] * routes.shape[1]
        whole = chips * cores * tokens.shape[0]
        if cores == 2 and chips % 2 == 0 and chips > 2 and whole <= 2 * slots:
            return ring_local(ring_of(mesh), tokens, cotangent, routes, *rest)
        return exchange_local(tokens, cotangent, routes, *rest)

    return jax.shard_map(
        local,
        mesh=mesh,
        in_specs=(
            P(("groups", "expert", "dp"), None),
            P(("groups", "expert", "dp"), None),
            P(("groups", "expert", "dp"), None),
            P(("groups", "expert", "dp"), None),
            P("groups"),
            P(("expert", "dp"), None, None),
            P(("expert", "dp"), None, None),
            P(("expert", "dp"), None, None),
        ),
        out_specs=(
            P(("groups", "expert", "dp"), None),
            P(("groups", "expert", "dp"), None, None),
            P(("groups", "expert", "dp"), None, None),
            P(("groups", "expert", "dp"), None, None),
        ),
        check_vma=False,
    )
```

```python
import functools

import jax
import jax.numpy as jnp
from jax import lax
from jax.experimental import pallas as pl
from jax.experimental.pallas import tpu as pltpu
from jax.sharding import PartitionSpec as P

OVER_LAST = (((1,), (1,)), ((), ()))
EXPERT_VMEM = 28 * 1024 * 1024
GRADS_VMEM = 24 * 1024 * 1024
CHEAP = pl.CostEstimate(flops=1024, bytes_accessed=1024, transcendentals=0)


def ring_of(mesh):
    chips = list(mesh.devices[0, :, 0])
    places = [getattr(chip, "coords", None) for chip in chips]
    natural = list(range(len(chips)))
    if any(place is None for place in places):
        return natural
    at = {(place[0], place[2]): i for i, place in enumerate(places)}
    xs = sorted({x for x, _ in at})
    zs = sorted({z for _, z in at})
    if len(at) != len(chips) or len(xs) * len(zs) != len(chips):
        return natural
    if len(xs) == 2:
        return [at[xs[0], z] for z in zs] + [at[xs[1], z] for z in reversed(zs)]
    if len(zs) == 2:
        return [at[x, zs[0]] for x in xs] + [at[x, zs[1]] for x in reversed(xs)]
    return natural


def pack_kernel(home_cap, lanes, routes_ref, gates_ref, helper_ref, tokens_ref, out_ref):
    rows, width = tokens_ref.shape
    experts = helper_ref.shape[1]
    expert_of_row = lax.broadcasted_iota(jnp.int32, (experts, rows), 0)
    named = jnp.zeros((experts, rows), jnp.float32)
    gate = jnp.zeros((experts, rows), jnp.float32)
    for k in range(routes_ref.shape[0]):
        hit = routes_ref[k : k + 1, :] == expert_of_row
        named = named + jnp.where(hit, 1.0, 0.0)
        gate = gate + jnp.where(hit, gates_ref[k : k + 1, :], 0.0)
    earlier = lax.broadcasted_iota(jnp.int32, (rows, rows), 0) < lax.broadcasted_iota(
        jnp.int32, (rows, rows), 1
    )
    rank = jnp.dot(
        named.astype(jnp.bfloat16),
        jnp.where(earlier, 1.0, 0.0).astype(jnp.bfloat16),
        preferred_element_type=jnp.float32,
    )
    partner = jnp.bitwise_xor(lax.broadcasted_iota(jnp.int32, (experts, experts), 0), 1)
    column = lax.broadcasted_iota(jnp.int32, (experts, experts), 1)
    flag = jnp.where(partner == column, helper_ref[...], 0)
    helped = jnp.max(flag, axis=1, keepdims=True) == 1
    gate = jnp.where((rank < home_cap) | helped, gate, 0.0)
    terms = []
    for _ in range(3):
        term = gate.astype(jnp.bfloat16).astype(jnp.float32)
        terms.append(term)
        gate = gate - term
    terms.append(jnp.zeros((lanes - 3 * experts, rows), jnp.float32))
    out_ref[:, :width] = tokens_ref[...]
    out_ref[:, width:] = jnp.concatenate(terms, axis=0).T.astype(jnp.bfloat16)


def pack(tokens, routes, gates, helper, home_cap):
    rows, width = tokens.shape
    lanes = 128 * pl.cdiv(3 * helper.shape[0] + 1, 128)
    return pl.pallas_call(
        functools.partial(pack_kernel, home_cap, lanes),
        out_shape=jax.ShapeDtypeStruct((rows, width + lanes), jnp.bfloat16),
        name="pack",
    )(routes.T, gates.T, helper[None, :], tokens)


def expert_kernel(count, experts, *refs):
    token_refs, cot_refs, sources = refs[:count], refs[count : 2 * count], refs[2 * count : 2 * count + 6]
    rest = refs[2 * count + 6 :]
    outs, rest = rest[: 5 + 2 * count], rest[5 + 2 * count :]
    held_tokens, held_cot, *weights = rest[:8]
    results, (arrived, left) = rest[8:-2], rest[-2:]
    turned, act_refs, hidden_refs, grad_refs = results[0], results[1:3], results[3:5], results[5:]
    rows, width = cot_refs[0].shape
    lanes = token_refs[0].shape[1] - width
    hidden = weights[0].shape[1]
    total = rows * count
    chip, core, cores = lax.axis_index("expert"), lax.axis_index("dp"), lax.axis_size("dp")
    ins = []
    for i in range(count):
        ins.append((token_refs[i], held_tokens.at[pl.ds(i * rows, rows)]))
    ins.append((sources[0], weights[0]))
    ins.append((sources[1], weights[1]))
    for i in range(count):
        ins.append((cot_refs[i], held_cot.at[pl.ds(i * rows, rows)]))
    ins += [(sources[i], weights[i]) for i in range(2, 6)]
    copies = [pltpu.make_async_copy(src, dst, arrived.at[i]) for i, (src, dst) in enumerate(ins)]
    soon = count + 2
    for copy in copies[:soon]:
        copy.start()
    pending = iter(copies)

    def wait(number):
        for _ in range(number):
            next(pending).wait()

    sends = [pltpu.make_async_copy(results[i], outs[i], left.at[i]) for i in range(len(outs))]
    lane = lax.broadcasted_iota(jnp.int32, (total, lanes), 1)
    wait(count)
    gate_terms = held_tokens[:, width:].astype(jnp.float32)
    grads = []
    for which in range(2):
        gate_w, up_w, down_w = weights[3 * which : 3 * which + 3]
        expert = chip * cores + (core if which == 0 else 1 - core)
        chosen = (lane == expert) | (lane == expert + experts) | (lane == expert + 2 * experts)
        gate = jnp.sum(jnp.where(chosen, gate_terms, 0.0), axis=1, keepdims=True)
        rows_in = held_tokens[:, :width]
        wait(1)
        if which == 0:
            for copy in copies[soon:]:
                copy.start()
        gate_pre = jnp.dot(rows_in, gate_w[...], preferred_element_type=jnp.float32)
        wait(1)
        up_pre = jnp.dot(rows_in, up_w[...], preferred_element_type=jnp.float32)
        wait(1 + count if which == 0 else 1)
        back = lax.dot_general(held_cot[...], down_w[...], OVER_LAST, preferred_element_type=jnp.float32)
        sigma = jax.nn.sigmoid(gate_pre)
        active = gate_pre * sigma
        back = back * gate
        grad_up = (back * active).astype(jnp.bfloat16)
        grad_gate = (back * up_pre * sigma * (1.0 + gate_pre * (1.0 - sigma))).astype(jnp.bfloat16)
        scaled_hidden = (active * up_pre * gate).astype(jnp.bfloat16)
        act_refs[which][:, :hidden] = grad_gate
        act_refs[which][:, hidden:] = grad_up
        hidden_refs[which][...] = scaled_hidden.T
        sends[1 + which].start()
        sends[3 + which].start()
        grads += [(grad_gate, gate_w), (grad_up, up_w)]
    step = 512
    cut = width // 2
    for part in range(2):
        for start in range(part * cut, part * cut + cut, step):
            sums = None
            for value, weight in grads:
                term = lax.dot_general(
                    value, weight[pl.ds(start, step), :], OVER_LAST, preferred_element_type=jnp.float32
                )
                sums = term if sums is None else sums + term
            turned[pl.ds(start, step), :] = held_tokens[:, pl.ds(start, step)].T
            for i in range(count):
                ref = grad_refs[2 * i + part]
                ref[:, pl.ds(start - part * cut, step)] = sums[i * rows : (i + 1) * rows].astype(ref.dtype)
        for i in range(count):
            sends[5 + 2 * i + part].start()
    sends[0].start()
    for send in sends:
        send.wait()


def expert_batch(blocks, weights, experts, grad_types):
    tokens, cots = zip(*blocks)
    rows, width = cots[0].shape
    hidden = weights[0].shape[1]
    total = rows * len(blocks)
    anywhere = pl.BlockSpec(memory_space=pl.ANY)
    half = jnp.bfloat16
    results = [((width, total), half)] + [((total, 2 * hidden), half)] * 2 + [((hidden, total), half)] * 2
    results += [((rows, width // 2), kind) for kind in grad_types]
    outs = pl.pallas_call(
        functools.partial(expert_kernel, len(blocks), experts),
        in_specs=[anywhere] * (2 * len(blocks) + 6),
        out_specs=[anywhere] * len(results),
        out_shape=[jax.ShapeDtypeStruct(shape, kind) for shape, kind in results],
        scratch_shapes=[
            pltpu.VMEM((total, tokens[0].shape[1]), half),
            pltpu.VMEM((total, width), half),
        ]
        + [pltpu.VMEM(weight.shape, half) for weight in weights]
        + [pltpu.VMEM(shape, kind) for shape, kind in results]
        + [
            pltpu.SemaphoreType.DMA((2 * len(blocks) + 6,)),
            pltpu.SemaphoreType.DMA((len(results),)),
        ],
        compiler_params=pltpu.CompilerParams(vmem_limit_bytes=EXPERT_VMEM),
        cost_estimate=CHEAP,
        name="expert_batch",
    )(*tokens, *cots, *weights)
    return outs[0], outs[1:3], outs[3:5], outs[5:]


def row_kernel(count, add, *refs):
    turned_refs, act_refs, rest = refs[:count], refs[count : 2 * count], refs[2 * count :]
    terms, outs, held = rest[:add], rest[add:-1], rest[-1]

    @pl.when(pl.program_id(0) == 0)
    def _():
        at = 0
        for ref in act_refs:
            held[pl.ds(at, ref.shape[0]), :] = ref[...]
            at += ref.shape[0]

    tile = jnp.concatenate([ref[...] for ref in turned_refs], axis=1)
    sums = jnp.dot(tile, held[...], preferred_element_type=jnp.float32)
    at = 0
    for i, ref in enumerate(outs):
        value = sums[:, at : at + ref.shape[1]]
        at += ref.shape[1]
        if add:
            value = value + terms[i][...].astype(jnp.float32)
        ref[...] = value.astype(jnp.bfloat16)


def row_grads(turned, acts, terms=()):
    width = turned[0].shape[0]
    hidden = acts[0].shape[1] // 2
    total = sum(act.shape[0] for act in acts)
    tile = 512
    out_spec = pl.BlockSpec((tile, hidden), lambda j: (j, 0))
    return pl.pallas_call(
        functools.partial(row_kernel, len(acts), len(terms)),
        grid=(width // tile,),
        in_specs=[pl.BlockSpec((tile, part.shape[1]), lambda j: (j, 0)) for part in turned]
        + [pl.BlockSpec(act.shape, lambda j: (0, 0)) for act in acts]
        + [out_spec] * len(terms),
        out_specs=[out_spec] * 2,
        out_shape=[jax.ShapeDtypeStruct((width, hidden), jnp.bfloat16)] * 2,
        scratch_shapes=[pltpu.VMEM((total, 2 * hidden), jnp.bfloat16)],
        compiler_params=pltpu.CompilerParams(vmem_limit_bytes=GRADS_VMEM),
        cost_estimate=CHEAP,
        name="row_grads",
    )(*turned, *acts, *terms)


def down_kernel(count, blocks, add, *refs):
    hidden_refs, cot_refs, rest = refs[:count], refs[count : count + blocks], refs[count + blocks :]
    terms, down_ref, held = rest[:add], rest[add], rest[-1]

    @pl.when(pl.program_id(0) == 0)
    def _():
        at = 0
        for ref in hidden_refs:
            held[:, pl.ds(at, ref.shape[1])] = ref[...]
            at += ref.shape[1]

    tile = jnp.concatenate([ref[...] for ref in cot_refs], axis=0)
    sums = jnp.dot(held[...], tile, preferred_element_type=jnp.float32)
    for term in terms:
        sums = sums + term[...].astype(jnp.float32)
    down_ref[...] = sums.astype(jnp.bfloat16)


def down_grads(hiddens, cots, terms=()):
    rows, width = cots[0].shape
    hidden = hiddens[0].shape[0]
    total = rows * len(cots)
    tile = 512
    out_spec = pl.BlockSpec((hidden, tile), lambda j: (0, j))
    return pl.pallas_call(
        functools.partial(down_kernel, len(hiddens), len(cots), len(terms)),
        grid=(width // tile,),
        in_specs=[pl.BlockSpec(part.shape, lambda j: (0, 0)) for part in hiddens]
        + [pl.BlockSpec((rows, tile), lambda j: (0, j))] * len(cots)
        + [out_spec] * len(terms),
        out_specs=out_spec,
        out_shape=jax.ShapeDtypeStruct((hidden, width), jnp.bfloat16),
        scratch_shapes=[pltpu.VMEM((hidden, total), jnp.bfloat16)],
        compiler_params=pltpu.CompilerParams(vmem_limit_bytes=GRADS_VMEM),
        cost_estimate=CHEAP,
        name="down_grads",
    )(*hiddens, *cots, *terms)


def ring_local(ring, tokens, cotangent, routes, gates, helper, w_gate, w_up, w_down):
    experts = helper.shape[0]
    chips, cores = lax.axis_size("expert"), lax.axis_size("dp")
    route_cap = 2 * tokens.shape[0] * routes.shape[1] // (chips * cores)
    home_cap = route_cap - 3 * route_cap // 8
    reach = chips // 2
    up_pairs = [(ring[i], ring[(i + 1) % chips]) for i in range(chips)]
    down_pairs = [(b, a) for a, b in up_pairs]
    swap = [(0, 1), (1, 0)]
    up = lambda value: lax.ppermute(value, "expert", up_pairs)
    down = lambda value: lax.ppermute(value, "expert", down_pairs)
    other = lambda value: lax.ppermute(value, "dp", swap)
    tied = lax.optimization_barrier
    wide, half = jnp.float32, jnp.bfloat16

    packed = pack(tokens, routes, gates, helper, home_cap)
    own = (w_gate[0], w_up[0], w_down[0])
    weights = own + tuple(other(value) for value in own)
    turned, acts, hiddens, cots = [], [], [], []

    def batch(blocks, grad_types):
        turn, act, hid, grads = expert_batch(blocks, weights, experts, grad_types)
        turned.append(turn)
        acts.append(act)
        hiddens.append(hid)
        cots.extend(cot for _, cot in blocks)
        return grads

    own_low, own_high = batch([(packed, cotangent)], (wide, wide))
    below_low, below_high, above_low, above_high = [], [], [], []
    tok_b = tok_a = packed
    cot_b = cot_a = cotangent
    for s in range(1, reach):
        cot_b, cot_a = up(cot_b), down(cot_a)
        tok_b, tok_a = up(tok_b), down(tok_a)
        tok_b, tok_a, turned[-1] = tied((tok_b, tok_a, turned[-1]))
        last = half if s == reach - 1 else wide
        parts = batch([(tok_b, cot_b), (tok_a, cot_a)], (wide, last, last, wide))
        for store, part in zip((below_low, below_high, above_low, above_high), parts):
            store.insert(0, part)

    plus = lambda value, term: (value.astype(wide) + term).astype(half)
    far_cot, far_tok = down(cot_a), up(tok_b)
    high_down, low_up = down(below_high[0]), up(above_low[0])
    far_tok, turned[-1] = tied((far_tok, turned[-1]))
    far_low, far_high = batch([(far_tok, far_cot)], (half, half))
    low_down, high_up = down(far_low), up(far_high)

    sent, out = {}, {}

    def far_rows():
        parts = row_grads(turned, [act[1] for act in acts])
        sent["gate"], sent["up"] = parts
        return parts[0]

    def far_down():
        part = down_grads([hid[1] for hid in hiddens], cots)
        sent["down"] = part
        return part

    def own_rows():
        terms = (sent["gate"], sent["up"])
        out["gate"], out["up"] = row_grads(turned, [act[0] for act in acts], terms)
        return out["gate"]

    def own_down():
        out["down"] = down_grads([hid[0] for hid in hiddens], cots, (sent["down"],))
        return out["down"]

    chores = [far_rows, far_down, own_down, own_rows]
    swapped = []

    def before_chore(first, second):
        first, second, turned[-1], cots[-1] = tied((first, second, turned[-1], cots[-1]))
        return first, second

    def after_chore(first, second):
        first, second, _ = tied((first, second, chores.pop(0)()))
        return first, second

    for s in range(reach - 1):
        more = s + 1 < reach - 1
        if more:
            high_down, low_up = plus(high_down, below_high[s + 1]), plus(low_up, above_low[s + 1])
            high_down, low_up = before_chore(high_down, low_up)
            high_down, low_up = down(high_down), up(low_up)
        if s > 0 and chores:
            low_down, high_up = after_chore(low_down, high_up)
        if s > 0 and more:
            low_down, high_up, high_down, low_up = tied((low_down, high_up, high_down, low_up))
        low_down, high_up = plus(low_down, below_low[s]), plus(high_up, above_high[s])
        low_down, high_up = before_chore(low_down, high_up)
        if len(chores) == 2 and not swapped:
            names = list(sent)
            low_down, high_up, parts = tied((low_down, high_up, tuple(sent[name] for name in names)))
            sent.update((name, other(part)) for name, part in zip(names, parts))
            swapped.append(True)
        low_down, high_up = down(low_down), up(high_up)
        if s == 0 and chores:
            high_down, low_up = after_chore(high_down, low_up)
    if not swapped:
        while len(chores) > 2:
            low_down, high_up = after_chore(low_down, high_up)
        sent.update((name, other(part)) for name, part in list(sent.items()))
    while chores:
        low_down, high_up = after_chore(low_down, high_up)

    grad_low = (own_low + low_down.astype(wide) + low_up.astype(wide)).astype(half)
    grad_high = (own_high + high_down.astype(wide) + high_up.astype(wide)).astype(half)
    grad_tokens = jnp.concatenate([grad_low, grad_high], axis=1)
    return (grad_tokens, out["gate"][None], out["up"][None], out["down"][None])


def expert_pass(rows, scaled, gate_w, up_w, down_w):
    gate_pre = jnp.dot(rows, gate_w, preferred_element_type=jnp.float32)
    up_pre = jnp.dot(rows, up_w, preferred_element_type=jnp.float32)
    sigma = jax.nn.sigmoid(gate_pre)
    active = gate_pre * sigma
    hidden = (active * up_pre).astype(jnp.bfloat16)
    over_last = (((1,), (1,)), ((), ()))
    over_rows = (((0,), (0,)), ((), ()))
    back_hidden = lax.dot_general(scaled, down_w, over_last, preferred_element_type=jnp.float32)
    grad_gating = (back_hidden * up_pre * sigma * (1.0 + gate_pre * (1.0 - sigma))).astype(
        jnp.bfloat16
    )
    grad_upward = (back_hidden * active).astype(jnp.bfloat16)
    grad_down = lax.dot_general(hidden, scaled, over_rows, preferred_element_type=jnp.float32)
    grad_gate = lax.dot_general(rows, grad_gating, over_rows, preferred_element_type=jnp.float32)
    grad_up = lax.dot_general(rows, grad_upward, over_rows, preferred_element_type=jnp.float32)
    row_grads = lax.dot_general(grad_gating, gate_w, over_last, preferred_element_type=jnp.float32)
    row_grads = row_grads + lax.dot_general(
        grad_upward, up_w, over_last, preferred_element_type=jnp.float32
    )
    return (row_grads.astype(jnp.bfloat16), grad_gate, grad_up, grad_down)


def exchange_local(tokens, cotangent, routes, gates, helper, w_gate, w_up, w_down):
    tok_rows, width = tokens.shape
    top_count = routes.shape[1]
    devices = lax.axis_size(("expert", "dp"))
    route_cap = 2 * tok_rows * top_count // devices
    spill_cap = 3 * route_cap // 8
    home_cap = route_cap - spill_cap
    block_rows = tok_rows * top_count
    slots = devices * route_cap
    flat_ids = routes.reshape(block_rows)
    experts_row = jnp.arange(devices, dtype=jnp.int32)
    one_hot = (flat_ids[:, None] == experts_row[None, :]).astype(jnp.float32)
    positions = jnp.arange(block_rows, dtype=jnp.int32)
    lower = (positions[:, None] > positions[None, :]).astype(jnp.float32)
    before = jnp.dot(lower, one_hot, precision=lax.Precision.HIGHEST)
    route_rank = jnp.sum(before * one_hot, axis=1).astype(jnp.int32)
    partner_help = helper.reshape(devices // 2, 2)[:, ::-1].reshape(devices).astype(jnp.float32)
    helped = jnp.dot(one_hot, partner_help, precision=lax.Precision.HIGHEST) > 0.5
    spilled = route_rank >= home_cap
    kept = jnp.logical_not(spilled) | helped
    slot_index = jnp.where(kept, flat_ids * route_cap + route_rank, slots)
    source = jnp.full((slots + 1,), block_rows, jnp.int32).at[slot_index].set(positions)[:slots]
    token_of = jnp.where(source < block_rows, source // top_count, tok_rows)
    tokens_pad = jnp.concatenate([tokens, jnp.zeros((1, width), jnp.bfloat16)], axis=0)
    cot_pad = jnp.concatenate([cotangent, jnp.zeros((1, width), jnp.bfloat16)], axis=0)
    gate_pad = jnp.concatenate([gates.reshape(block_rows), jnp.zeros((1,), jnp.float32)], axis=0)
    send_rows = tokens_pad[token_of].reshape(devices, route_cap, width)
    send_scaled = (cot_pad[token_of].astype(jnp.float32) * gate_pad[source][:, None]).astype(
        jnp.bfloat16
    )
    send_scaled = send_scaled.reshape(devices, route_cap, width)
    recv_rows, recv_scaled = (
        lax.all_to_all(send_rows, ("expert", "dp"), split_axis=0, concat_axis=0, tiled=True),
        lax.all_to_all(send_scaled, ("expert", "dp"), split_axis=0, concat_axis=0, tiled=True),
    )
    gate_w = w_gate[0]
    up_w = w_up[0]
    down_w = w_down[0]
    whole_out = expert_pass(
        recv_rows.reshape(slots, width), recv_scaled.reshape(slots, width), gate_w, up_w, down_w
    )
    grad_gate = whole_out[1]
    grad_up = whole_out[2]
    grad_down = whole_out[3]
    row_grads = whole_out[0].reshape(devices, route_cap, width)
    back_rows = lax.all_to_all(row_grads, ("expert", "dp"), split_axis=0, concat_axis=0, tiled=True)
    back_pad = jnp.concatenate(
        [back_rows.reshape(slots, width), jnp.zeros((1, width), jnp.bfloat16)], axis=0
    )
    picked = back_pad[slot_index].reshape(tok_rows, top_count, width)
    grad_tokens = jnp.sum(picked.astype(jnp.float32), axis=1).astype(jnp.bfloat16)
    return (
        grad_tokens,
        grad_gate[None].astype(jnp.bfloat16),
        grad_up[None].astype(jnp.bfloat16),
        grad_down[None].astype(jnp.bfloat16),
    )


def solution(mesh):
    chips, cores = mesh.shape["expert"], mesh.shape["dp"]

    def local(tokens, cotangent, routes, *rest):
        slots = 2 * tokens.shape[0] * routes.shape[1]
        whole = chips * cores * tokens.shape[0]
        if cores == 2 and chips % 2 == 0 and chips > 2 and whole <= 2 * slots:
            return ring_local(ring_of(mesh), tokens, cotangent, routes, *rest)
        return exchange_local(tokens, cotangent, routes, *rest)

    return jax.shard_map(
        local,
        mesh=mesh,
        in_specs=(
            P(("groups", "expert", "dp"), None),
            P(("groups", "expert", "dp"), None),
            P(("groups", "expert", "dp"), None),
            P(("groups", "expert", "dp"), None),
            P("groups"),
            P(("expert", "dp"), None, None),
            P(("expert", "dp"), None, None),
            P(("expert", "dp"), None, None),
        ),
        out_specs=(
            P(("groups", "expert", "dp"), None),
            P(("groups", "expert", "dp"), None, None),
            P(("groups", "expert", "dp"), None, None),
            P(("groups", "expert", "dp"), None, None),
        ),
        check_vma=False,
    )
```
